128 devices in a mesh: pipe: 2 (over core), expert: 8 (over y_lo, x), etp: 8 (over y_hi, z).
Axes of the slice: x: 4, y: 4 (y_hi: 2, y_lo: 2; y = y_hi * 2 + y_lo), z: 4, core: 2. Of those that a mesh axis runs over, the one named last changes fastest.
Arguments:
- tokens_in: bfloat16 [2, 1024, 3072], P('pipe', 'expert'), may hold values from -6 to 6
- cotangent_in: bfloat16 [2, 1024, 3072], P('pipe', 'expert'), may hold values from -6 to 6
- expert_ids: int32 [2, 1024, 2], P('pipe'), may hold values from 0 to 7, all different within a row; in each aligned block of 128 rows (0 to 127, 128 to 255, ..., all dimensions but the last counted through in order) at most 64 rows name the same one
- router_weight: bfloat16 [2, 3072, 8], P('pipe'), may hold values from -0.109375 to 0.109375
- gate_weight: bfloat16 [2, 8, 3072, 8192], P('pipe', 'expert', None, 'etp'), may hold values from -0.109375 to 0.109375
- up_weight: bfloat16 [2, 8, 3072, 8192], P('pipe', 'expert', None, 'etp'), may hold values from -0.109375 to 0.109375
- down_weight: bfloat16 [2, 8, 8192, 3072], P('pipe', 'expert', 'etp'), may hold values from -0.0625 to 0.0625
Outputs:
- layer_out: bfloat16 [2, 1024, 3072], P('pipe', ('expert', 'etp'))
- rows_grad: bfloat16 [2, 1024, 3072], P('pipe', ('expert', 'etp'))
The draws below stay inside these ranges and needn't reach their ends.
Inputs may be any that keep to these rules, and one draw needn't show every extreme that they name: `expert_ids`: the two experts of a token differ. In each aligned block of 128 rows (the tokens of one expert group) no expert is named more than 64 times, a bound that some block reaches.
All inputs are finite; a program needn't handle non-finite values.
Results may differ from the reference program's by a relative error of at most 0.0065.
Values may be sent and summed in bfloat16 or wider, within the bound.
No kernel may reach another device: no remote copies, remote signals or barrier semaphores. Data moves between devices by JAX's collectives and lax.ppermute only.
A program may use at most 192 MiB of HBM per device.

```python
import math
import jax
import jax.numpy as jnp
import numpy as np
from jax import lax

D = 3072
FF = 8192
TOK_DEV = 128
SECTIONS = 2
EXPERTS = 8
C_SRC = 64
TOKENS = 1024
CAP = 512


def levels(key, extent, pieces, low, largest):
    loudness, own = 1.0, jax.random.fold_in(key, 6)
    for position, shards_of in pieces:
        steps = jnp.exp(jax.random.uniform(jax.random.fold_in(own, position), (shards_of,), jnp.float32, low / len(pieces), largest / len(pieces)))
        loudness = loudness * jnp.repeat(steps, extent[position] // shards_of).reshape([-1 if axis == position else 1 for axis in range(len(extent))])
    return loudness


def routed_block(stream_key, own, number, rows, count, top, limit, slope):
    order = jax.random.permutation(stream_key, count)
    crowded, usual = shares(count, rows * top, limit, slope, True), shares(count, rows * top, limit, slope, False)
    places = jnp.arange(count)

    def named(lengths, rotation):
        used = int((lengths > 0).sum())
        fixed = max(1, used // 4)
        moved = fixed + (places - fixed + rotation * (used - fixed)) % max(1, count - fixed)
        return jnp.zeros((count,), jnp.int32).at[order[jnp.where(places < fixed, places, moved)]].set(jnp.asarray(lengths, jnp.int32))

    lengths = jnp.where(number % 4 == 0, named(crowded, number // 4), named(usual, number - number // 4 - 1))
    mixed = jax.random.permutation(jax.random.fold_in(own, 3), count)
    giver, receiver = mixed[0:count // 2 * 2:2], mixed[1:count // 2 * 2:2]
    slack = jnp.minimum(lengths[giver] - 1, limit - lengths[receiver]) // 2
    slack = jnp.where((giver == order[0]) | (receiver == order[0]) | (lengths[receiver] == 0), 0, jnp.maximum(slack, 0))
    moved = jax.random.randint(jax.random.fold_in(own, 4), (count // 2,), 0, 1 << 20) % (slack + 1)
    lengths = lengths.at[giver].add(-moved).at[receiver].add(moved)
    items = jnp.searchsorted(jnp.cumsum(lengths), jnp.arange(rows * top), side="right").astype(jnp.int32)
    table = items.reshape(top, rows).T
    table = table[jax.random.permutation(jax.random.fold_in(own, 1), rows)]
    rotation = jax.random.randint(jax.random.fold_in(own, 2), (rows, 1), 0, top)
    return jnp.take_along_axis(table, (jnp.arange(top)[None, :] + rotation) % top, axis=1)


def shares(number_of, total, most, lean, full):
    loads = [(1 << 20) // math.isqrt(grade ** lean) + 1 for grade in range(1, number_of + 1)]
    largest = most if full else min(most, max(-(-total // number_of), total * loads[0] // sum(loads)))
    least = 1 if total - largest >= number_of - 1 else 0
    counts, spare = [largest] + [least] * (number_of - 1), total - largest - least * (number_of - 1)
    while spare > 0:
        free = [i for i in range(1, number_of) if counts[i] < largest] or [i for i in range(1, number_of) if counts[i] < most]
        pool, remaining = sum([loads[i] for i in free]), spare
        for i in free:
            more = min(most - counts[i], max(1, remaining * loads[i] // pool), spare)
            counts[i] = counts[i] + more
            spare = spare - more
    return np.array(counts)


def scatter_about(rng, extent, spread, limit, shards=(), kind=jnp.bfloat16):
    gain = levels(rng, extent, shards, -0.22, 0.18) if shards else 1.0
    drawn = jax.random.normal(rng, extent, jnp.float32) * spread * gain
    return jnp.minimum(jnp.maximum(drawn, -limit), limit).astype(kind)


def setup_inputs(seed: int = 0) -> dict:
    key_of = jax.random.split(jax.random.key(seed), 8)
    tokens_in = scatter_about(key_of[0], (SECTIONS, TOKENS, D), 1.0, 6.0, ((0, 2), (1, 8)))
    cotangent_in = scatter_about(key_of[1], (SECTIONS, TOKENS, D), 1.0, 6.0, ((0, 2), (1, 8)))
    expert_ids_keys = jax.random.split(jax.random.fold_in(key_of[2], 1), SECTIONS * TOKENS // TOK_DEV)
    expert_ids_turns = jax.random.permutation(jax.random.fold_in(key_of[2], 3), SECTIONS * TOKENS // TOK_DEV)
    expert_ids = jax.vmap(lambda own, number: routed_block(jax.random.fold_in(key_of[2], 2), own, number, TOK_DEV, EXPERTS, 2, C_SRC, 2))(expert_ids_keys, expert_ids_turns).reshape((SECTIONS, TOKENS, 2))
    router_weight = scatter_about(key_of[3], (SECTIONS, D, EXPERTS), D ** -0.5, 0.109375, ((0, 2),))
    gate_weight = scatter_about(key_of[4], (SECTIONS, EXPERTS, D, FF), D ** -0.5, 0.109375, ((0, 2), (1, 8), (3, 8)))
    up_weight = scatter_about(key_of[5], (SECTIONS, EXPERTS, D, FF), D ** -0.5, 0.109375, ((0, 2), (1, 8), (3, 8)))
    down_weight = scatter_about(key_of[6], (SECTIONS, EXPERTS, FF, D), FF ** -0.5, 0.0625, ((0, 2), (1, 8), (2, 8)))
    return {"tokens_in": tokens_in, "cotangent_in": cotangent_in, "expert_ids": expert_ids, "router_weight": router_weight, "gate_weight": gate_weight, "up_weight": up_weight, "down_weight": down_weight}


def route_slots(routes, block_rows, capacity_src, experts):
    count = routes.shape[0]
    flat_ids = routes.reshape(count // block_rows, block_rows * 2)
    onehot = (flat_ids[:, :, None] == jnp.arange(experts, dtype=jnp.int32)[None, None, :]).astype(jnp.int32)
    before = jnp.cumsum(onehot, axis=1) - onehot
    rank_ids = lax.optimization_barrier(jnp.sum(before * onehot, axis=2))
    source = jnp.arange(count // block_rows, dtype=jnp.int32)[:, None]
    slot_ids = source * capacity_src + rank_ids
    return (slot_ids.reshape(count, 2).astype(jnp.int32), rank_ids.reshape(count, 2).astype(jnp.int32))

def pair_weights(scores, routes):
    chosen = jnp.take_along_axis(scores, routes, axis=1)
    score_gap = chosen[:, ::-1] - chosen
    return 1.0 / (1.0 + jnp.exp(score_gap))

def swish_parts(gate_pre):
    sigmoid_part = jax.nn.sigmoid(gate_pre)
    return (gate_pre * sigmoid_part, sigmoid_part * (1.0 + gate_pre * (1.0 - sigmoid_part)))

def expert_pass(expert_rows, scaled_cot, w_gate, w_up, w_down):
    gate_pre = jnp.dot(expert_rows, w_gate, preferred_element_type=jnp.float32)
    up_pre = jnp.dot(expert_rows, w_up, preferred_element_type=jnp.float32)
    swished, swish_slope = swish_parts(gate_pre)
    hidden = (swished * up_pre).astype(jnp.bfloat16)
    expert_out = jnp.dot(hidden, w_down, preferred_element_type=jnp.float32)
    d_hidden = jnp.dot(scaled_cot, w_down.T, preferred_element_type=jnp.float32)
    d_up = (d_hidden * swished).astype(jnp.bfloat16)
    d_gate = (d_hidden * up_pre * swish_slope).astype(jnp.bfloat16)
    d_rows = jnp.dot(d_gate, w_gate.T, preferred_element_type=jnp.float32)
    d_rows = d_rows + jnp.dot(d_up, w_up.T, preferred_element_type=jnp.float32)
    return (expert_out, d_rows)

def score_grad(weights, d_weights, routes, experts):
    d_left = weights[:, 0] * weights[:, 1] * (d_weights[:, 0] - d_weights[:, 1])
    columns = jnp.arange(experts, dtype=jnp.int32)[None, :]
    first = (routes[:, 0:1] == columns).astype(jnp.float32)
    second = (routes[:, 1:2] == columns).astype(jnp.float32)
    return ((first - second) * d_left[:, None]).astype(jnp.bfloat16)

def reference(tokens_in, cotangent_in, expert_ids, router_weight, gate_weight, up_weight, down_weight):
    arrived_all = jnp.roll(tokens_in, 1, axis=0)
    upstream_all = jnp.roll(cotangent_in, -1, axis=0)
    outputs = []
    gradients = []
    for section_index in range(SECTIONS):
        arrived = arrived_all[section_index]
        upstream = upstream_all[section_index]
        routes = expert_ids[section_index]
        router = router_weight[section_index]
        scores = jnp.dot(arrived, router, preferred_element_type=jnp.float32)
        weights = pair_weights(scores, routes)
        slot_ids, rank_ids = route_slots(routes, TOK_DEV, C_SRC, EXPERTS)
        token_of = jnp.repeat(jnp.arange(TOKENS, dtype=jnp.int32), 2)
        row_table = jnp.full((EXPERTS, CAP), TOKENS, jnp.int32).at[routes.reshape(-1), slot_ids.reshape(-1)].set(token_of)
        weight_table = jnp.zeros((EXPERTS, CAP), jnp.float32).at[routes.reshape(-1), slot_ids.reshape(-1)].set(weights.reshape(-1))
        arrived_pad = jnp.concatenate([arrived, jnp.zeros((1, D), jnp.bfloat16)], axis=0)
        upstream_pad = jnp.concatenate([upstream, jnp.zeros((1, D), jnp.bfloat16)], axis=0)

        def one_expert(expert_index):
            index_rows = row_table[expert_index]
            expert_rows = arrived_pad[index_rows]
            scaled_cot = (weight_table[expert_index][:, None] * upstream_pad[index_rows].astype(jnp.float32)).astype(jnp.bfloat16)
            return expert_pass(expert_rows, scaled_cot, gate_weight[section_index, expert_index], up_weight[section_index, expert_index], down_weight[section_index, expert_index])
        expert_out, d_expert = lax.map(one_expert, jnp.arange(EXPERTS, dtype=jnp.int32))
        chosen_rows = expert_out[routes, slot_ids]
        layer_rows = lax.optimization_barrier(jnp.sum(weights[:, :, None] * chosen_rows, axis=1)).astype(jnp.bfloat16)
        d_weights = lax.optimization_barrier(jnp.sum(upstream.astype(jnp.float32)[:, None, :] * chosen_rows, axis=2))
        d_scores = score_grad(weights, d_weights, routes, EXPERTS)
        grad_rows = lax.optimization_barrier(jnp.sum(d_expert[routes, slot_ids], axis=1))
        grad_rows = grad_rows + jnp.dot(d_scores, router.T, preferred_element_type=jnp.float32)
        outputs.append(layer_rows)
        gradients.append(grad_rows.astype(jnp.bfloat16))
    return (jnp.stack(outputs, axis=0), jnp.stack(gradients, axis=0))
```

```python
import functools

import jax
import jax.numpy as jnp
from jax import lax
from jax.experimental import pallas as pl
from jax.experimental.pallas import tpu as pltpu
from jax.sharding import PartitionSpec as P

F32 = jnp.float32
BF16 = jnp.bfloat16
SIDE = 4
VMEM_LIMIT = 56 * 1024 * 1024


def moved(x, axis, flip, by):
    pairs = [
        (hi * SIDE + lo, (hi ^ flip) * SIDE + (lo + by) % SIDE) for hi in range(2) for lo in range(SIDE)
    ]
    return lax.ppermute(x, axis, pairs)


def column_tile(width):
    return 512 if width % 512 == 0 else width


def slot_targets(pos_ref, row, slots):
    y_lo, x, z = pos_ref[1], pos_ref[2], pos_ref[3]
    quarter = slots // SIDE
    direct = y_lo * (SIDE * slots) + ((x + row // slots) % SIDE) * slots + row % slots
    rest = row - SIDE * slots
    cross = (1 - y_lo) * (SIDE * slots) + ((x + rest // quarter) % SIDE) * slots + z * quarter + rest % quarter
    target = jnp.where(row < SIDE * slots, direct, cross)
    return jnp.where(row < SIDE * slots + slots, target, -1)


def dispatch_kernel(slots, pos_ref, ids_ref, arrived_ref, upstream_ref, router_ref, meta_ref, *outs):
    rows_out, cot_out, cross_out = outs[:SIDE], outs[SIDE : 2 * SIDE], outs[2 * SIDE :]
    count, width = arrived_ref.shape
    experts = router_ref.shape[1]
    quarter = slots // SIDE
    ids = ids_ref[...]
    first, second = ids[:, 0:1], ids[:, 1:2]
    lane = lax.broadcasted_iota(jnp.int32, (count, count), 1)
    row = lax.broadcasted_iota(jnp.int32, (count, count), 0)
    pick0 = (lane == first).astype(F32)
    pick1 = (lane == second).astype(F32)
    below = (row > lane).astype(F32).astype(BF16)
    before = jnp.dot(below, (pick0 + pick1).astype(BF16), preferred_element_type=F32)
    slot0 = first.astype(F32) * slots + jnp.sum(before * pick0, axis=1, keepdims=True)
    slot1 = second.astype(F32) * slots + jnp.sum(before * pick1, axis=1, keepdims=True)
    scores = jnp.dot(arrived_ref[...], router_ref[...], preferred_element_type=F32)
    left = jnp.sum(scores * pick0[:, :experts], axis=1, keepdims=True)
    right = jnp.sum(scores * pick1[:, :experts], axis=1, keepdims=True)
    weight0 = 1.0 / (1.0 + jnp.exp(right - left))
    weight1 = 1.0 / (1.0 + jnp.exp(left - right))
    meta = jnp.where(lane == 0, slot0, 0.0)
    meta = jnp.where(lane == 1, slot1, meta)
    meta = jnp.where(lane == 2, weight0, meta)
    meta = jnp.where(lane == 3, weight1, meta)
    meta_ref[...] = meta
    flat = meta.T
    total = SIDE * slots + slots
    target = slot_targets(pos_ref, lax.broadcasted_iota(jnp.int32, (total, count), 0), slots).astype(F32)
    hit0 = (target == flat[0:1, :]).astype(F32)
    hit1 = (target == flat[1:2, :]).astype(F32)
    scale = jnp.sum(hit0 * flat[2:3, :] + hit1 * flat[3:4, :], axis=1, keepdims=True)
    hits = (hit0 + hit1).astype(BF16)
    tile = column_tile(width)
    for start in range(0, width, tile):
        columns = slice(start, start + tile)
        rows = jnp.dot(hits, arrived_ref[:, columns], preferred_element_type=F32).astype(BF16)
        cot = (scale * jnp.dot(hits, upstream_ref[:, columns], preferred_element_type=F32)).astype(BF16)
        for by in range(SIDE):
            part = slice(by * slots, (by + 1) * slots)
            rows_out[by][:, columns] = rows[part]
            cot_out[by][:, columns] = cot[part]
            part = slice(SIDE * slots + by * quarter, SIDE * slots + (by + 1) * quarter)
            cross_out[by][0:quarter, columns] = rows[part]
            cross_out[by][quarter : 2 * quarter, columns] = cot[part]


def dispatch(position, routes, arrived, upstream, router, slots):
    count, width = arrived.shape
    experts = router.shape[1]
    quarter = slots // SIDE
    whole = lambda *shape: pl.BlockSpec(shape, lambda i, pos: (0,) * len(shape))
    outs = (
        [jax.ShapeDtypeStruct((count, count), F32)]
        + [jax.ShapeDtypeStruct((slots, width), BF16)] * (2 * SIDE)
        + [jax.ShapeDtypeStruct((2 * quarter, width), BF16)] * SIDE
    )
    results = pl.pallas_call(
        functools.partial(dispatch_kernel, slots),
        out_shape=outs,
        grid_spec=pltpu.PrefetchScalarGridSpec(
            num_scalar_prefetch=1,
            grid=(1,),
            in_specs=[
                pl.BlockSpec((count, 2), lambda i, pos: (pos[0], 0)),
                whole(count, width),
                whole(count, width),
                whole(width, experts),
            ],
            out_specs=[whole(*out.shape) for out in outs],
        ),
        compiler_params=pltpu.CompilerParams(vmem_limit_bytes=VMEM_LIMIT),
        cost_estimate=pl.CostEstimate(
            flops=4 * 5 * slots * count * width, bytes_accessed=16 * count * width, transcendentals=0
        ),
        name="dispatch",
    )(position, routes, arrived, upstream, router)
    return results[0], results[1 : 1 + SIDE], results[1 + SIDE : 1 + 2 * SIDE], results[1 + 2 * SIDE :]


def load_chunks(chunks, rows_v, sems):
    size = chunks[0].shape[0]
    copies = [
        pltpu.make_async_copy(chunk, rows_v.at[pl.ds(k * size, size)], sems.at[k])
        for k, chunk in enumerate(chunks)
    ]
    for copy in copies:
        copy.start()
    for copy in copies:
        copy.wait()


def forward_kernel(n_chunks, hidden_steps, *refs):
    chunks, refs = refs[:n_chunks], refs[n_chunks:]
    gate_ref, up_ref, down_ref, refs = refs[0], refs[1], refs[2], refs[3:]
    outs, refs = refs[:n_chunks], refs[n_chunks:]
    swished_ref, slope_ref, rows_v, hidden_v, sems = refs
    step = pl.program_id(0)
    size = outs[0].shape[0]
    tile = gate_ref.shape[1]

    @pl.when(step == 0)
    def _():
        load_chunks(chunks, rows_v, sems)

    @pl.when(step < hidden_steps)
    def _():
        gate_pre = jnp.dot(rows_v[...], gate_ref[...], preferred_element_type=F32)
        up_pre = jnp.dot(rows_v[...], up_ref[...], preferred_element_type=F32)
        sigmoid_part = jax.nn.sigmoid(gate_pre)
        swished = gate_pre * sigmoid_part
        swished_ref[...] = swished
        slope_ref[...] = up_pre * (sigmoid_part * (1.0 + gate_pre * (1.0 - sigmoid_part)))
        hidden_v[:, pl.ds(pl.multiple_of(step * tile, tile), tile)] = (swished * up_pre).astype(BF16)

    @pl.when(step >= hidden_steps)
    def _():
        out = jnp.dot(hidden_v[...], down_ref[...], preferred_element_type=F32).astype(BF16)
        for k, ref in enumerate(outs):
            ref[...] = out[k * size : (k + 1) * size]


def forward(chunks, w_gate, w_up, w_down):
    size, width = chunks[0].shape
    rows = size * len(chunks)
    units = w_gate.shape[1]
    unit_tile = 256 if units % 256 == 0 else units
    tile = column_tile(width)
    hidden_steps, out_steps = units // unit_tile, width // tile
    early = lambda i: (0, jnp.minimum(i, hidden_steps - 1))
    late = lambda i: (0, jnp.maximum(i - hidden_steps, 0))
    results = pl.pallas_call(
        functools.partial(forward_kernel, len(chunks), hidden_steps),
        out_shape=[jax.ShapeDtypeStruct((size, width), BF16)] * len(chunks)
        + [jax.ShapeDtypeStruct((rows, units), F32)] * 2,
        grid=(hidden_steps + out_steps,),
        in_specs=[pl.BlockSpec(memory_space=pl.ANY)] * len(chunks)
        + [
            pl.BlockSpec((width, unit_tile), early),
            pl.BlockSpec((width, unit_tile), early),
            pl.BlockSpec((units, tile), late),
        ],
        out_specs=[pl.BlockSpec((size, tile), late)] * len(chunks)
        + [pl.BlockSpec((rows, unit_tile), early)] * 2,
        scratch_shapes=[
            pltpu.VMEM((rows, width), BF16),
            pltpu.VMEM((rows, units), BF16),
            pltpu.SemaphoreType.DMA((len(chunks),)),
        ],
        compiler_params=pltpu.CompilerParams(vmem_limit_bytes=VMEM_LIMIT),
        cost_estimate=pl.CostEstimate(
            flops=6 * rows * width * units,
            bytes_accessed=6 * width * units + 4 * rows * width + 8 * rows * units,
            transcendentals=rows * units,
        ),
        name="expert_forward",
    )(*chunks, w_gate, w_up, w_down)
    return results[: len(chunks)], results[-2], results[-1]


def transposed_dot(a, b):
    return lax.dot_general(a, b, (((1,), (1,)), ((), ())), preferred_element_type=F32)


def backward_kernel(n_chunks, hidden_steps, *refs):
    chunks, refs = refs[:n_chunks], refs[n_chunks:]
    swished_ref, slope_ref, gate_ref, up_ref, down_ref, refs = *refs[:5], refs[5:]
    outs, refs = refs[:n_chunks], refs[n_chunks:]
    cot_v, d_gate_v, d_up_v, sems = refs
    step = pl.program_id(0)
    size = outs[0].shape[0]
    tile = swished_ref.shape[1]

    @pl.when(step == 0)
    def _():
        load_chunks(chunks, cot_v, sems)

    @pl.when(step < hidden_steps)
    def _():
        d_hidden = transposed_dot(cot_v[...], down_ref[...])
        units = pl.ds(pl.multiple_of(step * tile, tile), tile)
        d_up_v[:, units] = (d_hidden * swished_ref[...]).astype(BF16)
        d_gate_v[:, units] = (d_hidden * slope_ref[...]).astype(BF16)

    @pl.when(step >= hidden_steps)
    def _():
        out = transposed_dot(d_gate_v[...], gate_ref[...]) + transposed_dot(d_up_v[...], up_ref[...])
        out = out.astype(BF16)
        for k, ref in enumerate(outs):
            ref[...] = out[k * size : (k + 1) * size]


def backward(chunks, swished, slope, w_gate, w_up, w_down):
    size, width = chunks[0].shape
    rows = size * len(chunks)
    units = w_gate.shape[1]
    unit_tile = 256 if units % 256 == 0 else units
    tile = column_tile(width)
    hidden_steps, out_steps = units // unit_tile, width // tile
    early = lambda i: jnp.minimum(i, hidden_steps - 1)
    late = lambda i: jnp.maximum(i - hidden_steps, 0)
    return pl.pallas_call(
        functools.partial(backward_kernel, len(chunks), hidden_steps),
        out_shape=[jax.ShapeDtypeStruct((size, width), BF16)] * len(chunks),
        grid=(hidden_steps + out_steps,),
        in_specs=[pl.BlockSpec(memory_space=pl.ANY)] * len(chunks)
        + [
            pl.BlockSpec((rows, unit_tile), lambda i: (0, early(i))),
            pl.BlockSpec((rows, unit_tile), lambda i: (0, early(i))),
            pl.BlockSpec((tile, units), lambda i: (late(i), 0)),
            pl.BlockSpec((tile, units), lambda i: (late(i), 0)),
            pl.BlockSpec((unit_tile, width), lambda i: (early(i), 0)),
        ],
        out_specs=[pl.BlockSpec((size, tile), lambda i: (0, late(i)))] * len(chunks),
        scratch_shapes=[
            pltpu.VMEM((rows, width), BF16),
            pltpu.VMEM((rows, units), BF16),
            pltpu.VMEM((rows, units), BF16),
            pltpu.SemaphoreType.DMA((len(chunks),)),
        ],
        compiler_params=pltpu.CompilerParams(vmem_limit_bytes=VMEM_LIMIT),
        cost_estimate=pl.CostEstimate(
            flops=6 * rows * width * units,
            bytes_accessed=6 * width * units + 4 * rows * width + 8 * rows * units,
            transcendentals=0,
        ),
        name="expert_backward",
    )(*chunks, swished, slope, w_gate, w_up, w_down)


def sum_kernel(*refs):
    parts, outs = refs[:SIDE], refs[SIDE:]
    total = parts[0][...].astype(F32)
    for part in parts[1:]:
        total = total + part[...].astype(F32)
    total = total.astype(BF16)
    size = outs[0].shape[0]
    for k, ref in enumerate(outs):
        ref[...] = total[k * size : (k + 1) * size]


def sum_quarters(parts):
    rows, width = parts[0].shape
    return pl.pallas_call(
        sum_kernel,
        out_shape=[jax.ShapeDtypeStruct((rows // SIDE, width), BF16)] * SIDE,
        compiler_params=pltpu.CompilerParams(vmem_limit_bytes=VMEM_LIMIT),
        cost_estimate=pl.CostEstimate(
            flops=4 * rows * width, bytes_accessed=10 * rows * width, transcendentals=0
        ),
        name="sum_quarters",
    )(*parts)


def combine_kernel(weighted, pos_ref, meta_ref, *refs):
    direct, cross, refs = refs[:SIDE], refs[SIDE : 2 * SIDE], refs[2 * SIDE :]
    slots, width = direct[0].shape
    count = meta_ref.shape[0]
    meta = meta_ref[...]
    padded = 6 * slots
    target = slot_targets(pos_ref, lax.broadcasted_iota(jnp.int32, (count, padded), 1), slots).astype(F32)
    hit0 = (target == meta[:, 0:1]).astype(F32)
    hit1 = (target == meta[:, 1:2]).astype(F32)
    out_ref = refs[-1]
    tile = column_tile(width)
    blank = jnp.zeros((slots, tile), BF16)
    dots0 = dots1 = jnp.zeros((count, 1), F32)
    for start in range(0, width, tile):
        columns = slice(start, start + tile)
        terms = jnp.concatenate([ref[:, columns] for ref in direct + cross] + [blank], axis=0)
        if weighted:
            rows0 = jnp.dot(hit0.astype(BF16), terms, preferred_element_type=F32)
            rows1 = jnp.dot(hit1.astype(BF16), terms, preferred_element_type=F32)
            out_ref[:, columns] = (meta[:, 2:3] * rows0 + meta[:, 3:4] * rows1).astype(BF16)
            upstream = refs[0][:, columns].astype(F32)
            dots0 = dots0 + jnp.sum(upstream * rows0, axis=1, keepdims=True)
            dots1 = dots1 + jnp.sum(upstream * rows1, axis=1, keepdims=True)
        else:
            out_ref[:, columns] = jnp.dot((hit0 + hit1).astype(BF16), terms, preferred_element_type=F32).astype(BF16)
    if weighted:
        lane = lax.broadcasted_iota(jnp.int32, (count, 128), 1)
        high0, high1 = dots0.astype(BF16).astype(F32), dots1.astype(BF16).astype(F32)
        extra = jnp.where(lane == 0, high0, 0.0)
        extra = jnp.where(lane == 1, dots0 - high0, extra)
        extra = jnp.where(lane == 2, high1, extra)
        extra = jnp.where(lane == 3, dots1 - high1, extra)
        out_ref[:, width : width + 128] = extra.astype(BF16)


def combine(position, meta, direct, cross, upstream=None):
    weighted = upstream is not None
    slots, width = direct[0].shape
    count = meta.shape[0]
    vmem = pl.BlockSpec(memory_space=pltpu.VMEM)
    extra = [upstream] if weighted else []
    return pl.pallas_call(
        functools.partial(combine_kernel, weighted),
        out_shape=jax.ShapeDtypeStruct((count, width + (128 if weighted else 0)), BF16),
        in_specs=[pl.BlockSpec(memory_space=pltpu.SMEM)] + [vmem] * (1 + 2 * SIDE + len(extra)),
        out_specs=vmem,
        compiler_params=pltpu.CompilerParams(vmem_limit_bytes=VMEM_LIMIT),
        cost_estimate=pl.CostEstimate(
            flops=4 * count * 6 * slots * width, bytes_accessed=10 * slots * width + 4 * count * width, transcendentals=0
        ),
        name="combine",
    )(position, meta, *direct, *cross, *extra)


def finish_kernel(pos_ref, meta_ref, ids_ref, router_ref, out_ref, grad_ref, layer_ref, rows_ref):
    share = meta_ref.shape[0]
    width = layer_ref.shape[1]
    parts = out_ref.shape[0] // share
    total = out_ref[0:share, :].astype(F32)
    grads = grad_ref[0:share, :].astype(F32)
    for k in range(1, parts):
        total = total + out_ref[k * share : (k + 1) * share, :].astype(F32)
        grads = grads + grad_ref[k * share : (k + 1) * share, :].astype(F32)
    layer_ref[...] = total[:, :width].astype(BF16)
    extra = total[:, width : width + 128]
    d_gap = (extra[:, 0:1] + extra[:, 1:2]) - (extra[:, 2:3] + extra[:, 3:4])
    meta = meta_ref[...]
    d_left = meta[:, 2:3] * meta[:, 3:4] * d_gap
    d_left = d_left.astype(BF16).astype(F32)
    ids = ids_ref[...]
    for e in range(router_ref.shape[0]):
        sign = (ids[:, 0:1] == e).astype(F32) - (ids[:, 1:2] == e).astype(F32)
        grads = grads + (sign * d_left) * router_ref[e : e + 1, :]
    rows_ref[...] = grads.astype(BF16)


def finish(position, meta, routes, router_rows, out_parts, grad_parts, share):
    count, width = grad_parts.shape
    whole = lambda *shape: pl.BlockSpec(shape, lambda i, pos: (0,) * len(shape))
    return pl.pallas_call(
        finish_kernel,
        out_shape=[jax.ShapeDtypeStruct((share, width), BF16)] * 2,
        grid_spec=pltpu.PrefetchScalarGridSpec(
            num_scalar_prefetch=1,
            grid=(1,),
            in_specs=[
                pl.BlockSpec((share, meta.shape[1]), lambda i, pos: (pos[4], 0)),
                pl.BlockSpec((share, 2), lambda i, pos: (pos[5], 0)),
                whole(*router_rows.shape),
                whole(*out_parts.shape),
                whole(*grad_parts.shape),
            ],
            out_specs=[whole(share, width)] * 2,
        ),
        compiler_params=pltpu.CompilerParams(vmem_limit_bytes=VMEM_LIMIT),
        cost_estimate=pl.CostEstimate(flops=30 * count * width, bytes_accessed=4 * count * width, transcendentals=0),
        name="finish",
    )(position, meta, routes, router_rows, out_parts, grad_parts)


def exchange(x, axis):
    parts = lax.axis_size(axis)
    blocks = x.reshape(parts, x.shape[0] // parts, x.shape[1])
    return lax.all_to_all(blocks, axis, 0, 0).reshape(x.shape)


def gather_quarters(block):
    return [block] + [moved(block, "etp", 0, by) for by in range(1, SIDE)]


def send_back(chunks):
    direct, quarters = chunks[:SIDE], chunks[SIDE:]
    direct = [direct[0]] + [moved(direct[by], "expert", 0, -by) for by in range(1, SIDE)]
    quarters = [quarters[0]] + [moved(quarters[by], "etp", 0, -by) for by in range(1, SIDE)]
    cross = sum_quarters(quarters)
    cross = [moved(cross[by], "expert", 1, -by) for by in range(SIDE)]
    return direct, cross


def per_device(
    tokens_in, cotangent_in, expert_ids, router_weight, gate_weight, up_weight, down_weight
):
    swap = [(0, 1), (1, 0)]
    arrived = lax.ppermute(tokens_in[0], "pipe", swap)
    upstream = lax.ppermute(cotangent_in[0], "pipe", swap)
    routes = expert_ids[0]
    router = router_weight[0]
    w_gate = gate_weight[0, 0]
    w_up = up_weight[0, 0]
    w_down = down_weight[0, 0]
    count = arrived.shape[0]
    n_etp = lax.axis_size("etp")
    slots = 4 * count // lax.axis_size("expert")
    quarter = slots // SIDE
    share = count // n_etp
    group = lax.axis_index("expert")
    part = lax.axis_index("etp")
    position = jnp.stack([group, group // SIDE, group % SIDE, part % SIDE, part, group * n_etp + part]).astype(jnp.int32)
    meta, rows, cot, cross = dispatch(position, routes, arrived, upstream, router, slots)
    cross = [moved(cross[by], "expert", 1, by) for by in range(SIDE)]
    rows_direct = [rows[0]] + [moved(rows[by], "expert", 0, by) for by in range(1, SIDE)]
    rows_cross = gather_quarters(jnp.concatenate([c[:quarter] for c in cross], axis=0))
    cot_direct = [cot[0]] + [moved(cot[by], "expert", 0, by) for by in range(1, SIDE)]
    cot_cross = gather_quarters(jnp.concatenate([c[quarter:] for c in cross], axis=0))
    out_chunks, swished, slope = forward(rows_direct + rows_cross, w_gate, w_up, w_down)
    grad_chunks = backward(cot_direct + cot_cross, swished, slope, w_gate, w_up, w_down)
    out_direct, out_cross = send_back(out_chunks)
    out_terms = combine(position, meta, out_direct, out_cross, upstream)
    out_parts = exchange(out_terms, "etp")
    grad_direct, grad_cross = send_back(grad_chunks)
    grad_terms = combine(position, meta, grad_direct, grad_cross)
    grad_parts = exchange(grad_terms, "etp")
    router_rows = router.T.astype(F32)
    layer_rows, grad_rows = finish(position, meta, routes, router_rows, out_parts, grad_parts, share)
    return (layer_rows[None], grad_rows[None])


def solution(mesh):
    return jax.shard_map(
        per_device,
        mesh=mesh,
        in_specs=(
            P("pipe", "expert", None),
            P("pipe", "expert", None),
            P("pipe", None, None),
            P("pipe", None, None),
            P("pipe", "expert", None, "etp"),
            P("pipe", "expert", None, "etp"),
            P("pipe", "expert", "etp", None),
        ),
        out_specs=(P("pipe", ("expert", "etp"), None), P("pipe", ("expert", "etp"), None)),
        check_vma=False,
    )
```

```python
import functools

import jax
import jax.numpy as jnp
from jax import lax
from jax.experimental import pallas as pl
from jax.experimental.pallas import tpu as pltpu
from jax.sharding import PartitionSpec as P

F32 = jnp.float32
BF16 = jnp.bfloat16
SIDE = 4
STEPS = (0, 1, SIDE - 1, 2)
FORWARD_TILES = (256, 1024)
BACKWARD_TILES = (512, 512)
AHEAD = 2
VMEM_LIMIT = 56 * 1024 * 1024


def moved(x, axis, by):
    pairs = [(hi * SIDE + lo, hi * SIDE + (lo + by) % SIDE) for hi in range(2) for lo in range(SIDE)]
    return lax.ppermute(x, axis, pairs)


def exchange(x, axis, low=False):
    size = lax.axis_size(axis)
    groups = [list(range(start, start + SIDE)) for start in range(0, size, SIDE)] if low else None
    parts = SIDE if low else size
    blocks = x.reshape(parts, x.shape[0] // parts, x.shape[1])
    return lax.all_to_all(blocks, axis, 0, 0, axis_index_groups=groups).reshape(x.shape)


def column_tile(width):
    return 512 if width % 512 == 0 else width


def slot_targets(pos_ref, row, slots):
    y_lo, x, z = pos_ref[1], pos_ref[2], pos_ref[3]
    quarter = slots // SIDE
    head = 2 * SIDE * quarter
    expert = row // quarter
    first = expert * slots + jnp.where(expert // SIDE == y_lo, 0, z * quarter) + row % quarter
    rest = row - head
    more = slots - quarter
    second = (y_lo * SIDE + (x + rest // more) % SIDE) * slots + quarter + rest % more
    target = jnp.where(row < head, first, second)
    return jnp.where(row < head + SIDE * more, target, -1)


def route_kernel(slots, pos_ref, ids_ref, arrived_ref, router_ref, meta_ref, *refs):
    count, width = arrived_ref.shape
    experts = router_ref.shape[0]
    ids = jnp.concatenate([ids_ref[...].astype(F32), jnp.zeros((count - 2, count), F32)], axis=0).T.astype(jnp.int32)
    first, second = ids[:, 0:1], ids[:, 1:2]
    lane = lax.broadcasted_iota(jnp.int32, (count, count), 1)
    row = lax.broadcasted_iota(jnp.int32, (count, count), 0)
    pick0 = (lane == first).astype(F32)
    pick1 = (lane == second).astype(F32)
    below = (row > lane).astype(F32).astype(BF16)
    before = jnp.dot(below, (pick0 + pick1).astype(BF16), preferred_element_type=F32)
    slot0 = first.astype(F32) * slots + jnp.sum(before * pick0, axis=1, keepdims=True)
    slot1 = second.astype(F32) * slots + jnp.sum(before * pick1, axis=1, keepdims=True)
    scores = transposed_dot(arrived_ref[...], router_ref[...])
    left = jnp.sum(scores * pick0[:, :experts], axis=1, keepdims=True)
    right = jnp.sum(scores * pick1[:, :experts], axis=1, keepdims=True)
    weight0 = 1.0 / (1.0 + jnp.exp(right - left))
    weight1 = 1.0 / (1.0 + jnp.exp(left - right))
    meta = jnp.where(lane == 0, slot0, 0.0)
    meta = jnp.where(lane == 1, slot1, meta)
    meta = jnp.where(lane == 2, weight0, meta)
    meta = jnp.where(lane == 3, weight1, meta)
    meta_ref[...] = meta
    hits, _ = dispatch_hits(slots, pos_ref, meta)
    write_rows(hits, None, arrived_ref, refs)


def dispatch_hits(slots, pos_ref, meta):
    count = meta.shape[0]
    total = 2 * slots + SIDE * (slots - slots // SIDE)
    flat = meta.T
    target = slot_targets(pos_ref, lax.broadcasted_iota(jnp.int32, (total, count), 0), slots).astype(F32)
    hit0 = (target == flat[0:1, :]).astype(F32)
    hit1 = (target == flat[1:2, :]).astype(F32)
    scale = jnp.sum(hit0 * flat[2:3, :] + hit1 * flat[3:4, :], axis=1, keepdims=True)
    return (hit0 + hit1).astype(BF16), scale


def write_rows(hits, scale, source_ref, refs):
    width = source_ref.shape[1]
    tile = column_tile(width)
    for start in range(0, width, tile):
        columns = slice(start, start + tile)
        rows = jnp.dot(hits, source_ref[:, columns], preferred_element_type=F32)
        if scale is not None:
            rows = scale * rows
        write_chunks(rows.astype(BF16), [ref.at[:, columns] for ref in refs])


def cot_kernel(slots, pos_ref, meta_ref, upstream_ref, *refs):
    hits, scale = dispatch_hits(slots, pos_ref, meta_ref[...])
    write_rows(hits, scale, upstream_ref, refs)


def dispatch_shapes(slots, width):
    return [jax.ShapeDtypeStruct((2 * slots, width), BF16)] + [
        jax.ShapeDtypeStruct((slots - slots // SIDE, width), BF16)
    ] * SIDE


def dispatch_rows(position, routes, arrived, router, slots):
    count, width = arrived.shape
    whole = lambda *shape: pl.BlockSpec(shape, lambda i, pos: (0,) * len(shape))
    outs = [jax.ShapeDtypeStruct((count, count), F32)] + dispatch_shapes(slots, width)
    return pl.pallas_call(
        functools.partial(route_kernel, slots),
        out_shape=outs,
        grid_spec=pltpu.PrefetchScalarGridSpec(
            num_scalar_prefetch=1,
            grid=(1,),
            in_specs=[
                pl.BlockSpec((2, count), lambda i, pos: (0, pos[0])),
                whole(count, width),
                whole(*router.shape),
            ],
            out_specs=[whole(*out.shape) for out in outs],
        ),
        compiler_params=pltpu.CompilerParams(vmem_limit_bytes=VMEM_LIMIT),
        cost_estimate=pl.CostEstimate(
            flops=2 * 5 * slots * count * width, bytes_accessed=8 * count * width, transcendentals=0
        ),
        name="dispatch_rows",
    )(position, routes, arrived, router)


def dispatch_cot(position, meta, upstream, slots):
    count, width = upstream.shape
    whole = lambda *shape: pl.BlockSpec(shape, lambda i, pos: (0,) * len(shape))
    outs = dispatch_shapes(slots, width)
    return pl.pallas_call(
        functools.partial(cot_kernel, slots),
        out_shape=outs,
        grid_spec=pltpu.PrefetchScalarGridSpec(
            num_scalar_prefetch=1,
            grid=(1,),
            in_specs=[whole(*meta.shape), whole(count, width)],
            out_specs=[whole(*out.shape) for out in outs],
        ),
        compiler_params=pltpu.CompilerParams(vmem_limit_bytes=VMEM_LIMIT),
        cost_estimate=pl.CostEstimate(
            flops=2 * 5 * slots * count * width, bytes_accessed=8 * count * width, transcendentals=0
        ),
        name="dispatch_cot",
    )(position, meta, upstream)


def chunk_places(pos_ref, slots, apart):
    more = slots - slots // SIDE
    places = [(k * more, more) for k in range(SIDE)] + [(SIDE * more, slots)]
    base = SIDE * more + slots
    if not apart:
        return places + [(base, SIDE * slots)]
    z = pos_ref[3]
    return places + [(pl.multiple_of(base + lax.rem(z + SIDE - by, SIDE) * slots, slots), slots) for by in STEPS]


def chunk_shapes(slots, width, apart):
    sizes = [slots - slots // SIDE] * SIDE + [slots] + ([slots] * SIDE if apart else [SIDE * slots])
    return [jax.ShapeDtypeStruct((size, width), BF16) for size in sizes]


def row_copies(places, refs, rows_v, sems):
    return [
        pltpu.make_async_copy(ref, rows_v.at[pl.ds(start, size)], sems.at[k])
        for k, ((start, size), ref) in enumerate(zip(places, refs))
    ]


def result_copies(places, rows_v, columns, refs, sems):
    return [
        pltpu.make_async_copy(rows_v.at[pl.ds(start, size), columns], ref.at[:, columns], sems.at[k])
        for k, ((start, size), ref) in enumerate(zip(places, refs))
    ]


def tiles(extent, size):
    size = size if extent % size == 0 else extent
    return [pl.ds(start, size) for start in range(0, extent, size)]


def begin(copies):
    for copy in copies:
        copy.start()


def finish_copies(copies):
    for copy in copies:
        copy.wait()


def write_chunks(out, refs):
    start = 0
    for ref in refs:
        size = ref.shape[0]
        ref[...] = out[start : start + size]
        start += size


def forward_kernel(slots, pos_ref, *refs):
    places_in, places_out = chunk_places(pos_ref, slots, True), chunk_places(pos_ref, slots, False)
    chunks, refs = refs[: len(places_in)], refs[len(places_in) :]
    (gate, up, down), refs = refs[:3], refs[3:]
    outs, refs = refs[: len(places_out)], refs[len(places_out) :]
    (swished, slope), refs = refs[:2], refs[2:]
    rows_v, gate_v, up_v, down_v, gate_pre, up_pre, swished_v, slope_v, hidden_v, out_v, *sems = refs
    row_sem, gate_sem, up_sem, down_sem, swished_sem, slope_sem, out_sem = sems
    units, width = down.shape
    unit_tiles, column_tiles = tiles(units, FORWARD_TILES[0]), tiles(width, FORWARD_TILES[1])
    loads = []
    for k, part in enumerate(unit_tiles):
        loads.append(
            [
                pltpu.make_async_copy(gate.at[:, part], gate_v.at[:, part], gate_sem.at[k]),
                pltpu.make_async_copy(up.at[:, part], up_v.at[:, part], up_sem.at[k]),
            ]
        )
    for k, part in enumerate(column_tiles):
        loads.append([pltpu.make_async_copy(down.at[:, part], down_v.at[:, part], down_sem.at[k])])
    saves = []

    def activate(k):
        part = unit_tiles[k]
        gates, ups = gate_pre[k % 2], up_pre[k % 2]
        sigmoid_part = jax.nn.sigmoid(gates)
        swish = gates * sigmoid_part
        swished_v[:, part] = swish
        slope_v[:, part] = ups * (sigmoid_part * (1.0 + gates * (1.0 - sigmoid_part)))
        hidden_v[:, part] = (swish * ups).astype(BF16)

    def save(k):
        part = unit_tiles[k]
        copies = [
            pltpu.make_async_copy(swished_v.at[:, part], swished.at[:, part], swished_sem.at[k]),
            pltpu.make_async_copy(slope_v.at[:, part], slope.at[:, part], slope_sem.at[k]),
        ]
        begin(copies)
        saves.extend(copies)

    rows = row_copies(places_in, chunks, rows_v, row_sem)
    begin(rows)
    for k in range(AHEAD):
        begin(loads[k])
    finish_copies(rows)
    for k, part in enumerate(unit_tiles):
        finish_copies(loads[k])
        if k + AHEAD < len(loads):
            begin(loads[k + AHEAD])
        gate_pre[k % 2] = jnp.dot(rows_v[...], gate_v[:, part], preferred_element_type=F32)
        up_pre[k % 2] = jnp.dot(rows_v[...], up_v[:, part], preferred_element_type=F32)
        if k > 0:
            activate(k - 1)
            save(k - 1)
    activate(len(unit_tiles) - 1)
    save(len(unit_tiles) - 1)
    for k, part in enumerate(column_tiles):
        at = len(unit_tiles) + k
        finish_copies(loads[at])
        if at + AHEAD < len(loads):
            begin(loads[at + AHEAD])
        out_v[:, part] = jnp.dot(hidden_v[...], down_v[:, part], preferred_element_type=F32).astype(BF16)
        copies = result_copies(places_out, out_v, part, outs, out_sem.at[k])
        begin(copies)
        saves.extend(copies)
    finish_copies(saves)


def forward(position, chunks, w_gate, w_up, w_down, slots):
    width, units = w_gate.shape
    outs = chunk_shapes(slots, width, False)
    rows = sum(out.shape[0] for out in outs)
    unit_tiles, column_tiles = tiles(units, FORWARD_TILES[0]), tiles(width, FORWARD_TILES[1])
    unit_tile = unit_tiles[0].size
    anywhere = pl.BlockSpec(memory_space=pl.ANY)
    dma = pltpu.SemaphoreType.DMA
    results = pl.pallas_call(
        functools.partial(forward_kernel, slots),
        out_shape=outs + [jax.ShapeDtypeStruct((rows, units), F32)] * 2,
        in_specs=[pl.BlockSpec(memory_space=pltpu.SMEM)] + [anywhere] * (len(chunks) + 3),
        out_specs=[anywhere] * (len(outs) + 2),
        scratch_shapes=[
            pltpu.VMEM((rows, width), BF16),
            pltpu.VMEM((width, units), BF16),
            pltpu.VMEM((width, units), BF16),
            pltpu.VMEM((units, width), BF16),
            pltpu.VMEM((2, rows, unit_tile), F32),
            pltpu.VMEM((2, rows, unit_tile), F32),
            pltpu.VMEM((rows, units), F32),
            pltpu.VMEM((rows, units), F32),
            pltpu.VMEM((rows, units), BF16),
            pltpu.VMEM((rows, width), BF16),
            dma((len(chunks),)),
            dma((len(unit_tiles),)),
            dma((len(unit_tiles),)),
            dma((len(column_tiles),)),
            dma((len(unit_tiles),)),
            dma((len(unit_tiles),)),
            dma((len(column_tiles), len(outs))),
        ],
        compiler_params=pltpu.CompilerParams(vmem_limit_bytes=VMEM_LIMIT),
        cost_estimate=pl.CostEstimate(
            flops=6 * rows * width * units,
            bytes_accessed=6 * width * units + 4 * rows * width + 8 * rows * units,
            transcendentals=rows * units,
        ),
        name="expert_forward",
    )(position, *chunks, w_gate, w_up, w_down)
    return results


def transposed_dot(a, b):
    return lax.dot_general(a, b, (((1,), (1,)), ((), ())), preferred_element_type=F32)


def backward_kernel(slots, pos_ref, *refs):
    places_in, places_out = chunk_places(pos_ref, slots, False), chunk_places(pos_ref, slots, True)
    chunks, refs = refs[: len(places_in)], refs[len(places_in) :]
    (swished, slope, gate, up, down), refs = refs[:5], refs[5:]
    outs, refs = refs[: len(places_out)], refs[len(places_out) :]
    cot_v, gate_v, up_v, down_v, swished_v, slope_v, d_hidden, d_gate, d_up, out_v, *sems = refs
    row_sem, gate_sem, up_sem, down_sem, swished_sem, slope_sem, out_sem = sems
    units, width = down.shape
    unit_tiles, column_tiles = tiles(units, BACKWARD_TILES[0]), tiles(width, BACKWARD_TILES[1])
    loads = []
    for k, part in enumerate(unit_tiles):
        loads.append(
            [
                pltpu.make_async_copy(down.at[part], down_v.at[part], down_sem.at[k]),
                pltpu.make_async_copy(swished.at[:, part], swished_v.at[:, part], swished_sem.at[k]),
                pltpu.make_async_copy(slope.at[:, part], slope_v.at[:, part], slope_sem.at[k]),
            ]
        )
    for k, part in enumerate(column_tiles):
        loads.append(
            [
                pltpu.make_async_copy(gate.at[part], gate_v.at[part], gate_sem.at[k]),
                pltpu.make_async_copy(up.at[part], up_v.at[part], up_sem.at[k]),
            ]
        )
    saves = []

    def activate(k):
        part = unit_tiles[k]
        d_up[:, part] = (d_hidden[k % 2] * swished_v[:, part]).astype(BF16)
        d_gate[:, part] = (d_hidden[k % 2] * slope_v[:, part]).astype(BF16)

    rows = row_copies(places_in, chunks, cot_v, row_sem)
    begin(rows)
    for k in range(AHEAD):
        begin(loads[k])
    finish_copies(rows)
    for k, part in enumerate(unit_tiles):
        finish_copies(loads[k])
        if k + AHEAD < len(loads):
            begin(loads[k + AHEAD])
        d_hidden[k % 2] = transposed_dot(cot_v[...], down_v[part, :])
        if k > 0:
            activate(k - 1)
    activate(len(unit_tiles) - 1)
    for k, part in enumerate(column_tiles):
        at = len(unit_tiles) + k
        finish_copies(loads[at])
        if at + AHEAD < len(loads):
            begin(loads[at + AHEAD])
        out = transposed_dot(d_gate[...], gate_v[part, :]) + transposed_dot(d_up[...], up_v[part, :])
        out_v[:, part] = out.astype(BF16)
        copies = result_copies(places_out, out_v, part, outs, out_sem.at[k])
        begin(copies)
        saves.extend(copies)
    finish_copies(saves)


def backward(position, chunks, swished, slope, w_gate, w_up, w_down, slots):
    width, units = w_gate.shape
    outs = chunk_shapes(slots, width, True)
    rows = sum(out.shape[0] for out in outs)
    unit_tiles, column_tiles = tiles(units, BACKWARD_TILES[0]), tiles(width, BACKWARD_TILES[1])
    anywhere = pl.BlockSpec(memory_space=pl.ANY)
    dma = pltpu.SemaphoreType.DMA
    return pl.pallas_call(
        functools.partial(backward_kernel, slots),
        out_shape=outs,
        in_specs=[pl.BlockSpec(memory_space=pltpu.SMEM)] + [anywhere] * (len(chunks) + 5),
        out_specs=[anywhere] * len(outs),
        scratch_shapes=[
            pltpu.VMEM((rows, width), BF16),
            pltpu.VMEM((width, units), BF16),
            pltpu.VMEM((width, units), BF16),
            pltpu.VMEM((units, width), BF16),
            pltpu.VMEM((rows, units), F32),
            pltpu.VMEM((rows, units), F32),
            pltpu.VMEM((2, rows, unit_tiles[0].size), F32),
            pltpu.VMEM((rows, units), BF16),
            pltpu.VMEM((rows, units), BF16),
            pltpu.VMEM((rows, width), BF16),
            dma((len(chunks),)),
            dma((len(column_tiles),)),
            dma((len(column_tiles),)),
            dma((len(unit_tiles),)),
            dma((len(unit_tiles),)),
            dma((len(unit_tiles),)),
            dma((len(column_tiles), len(outs))),
        ],
        compiler_params=pltpu.CompilerParams(vmem_limit_bytes=VMEM_LIMIT),
        cost_estimate=pl.CostEstimate(
            flops=6 * rows * width * units,
            bytes_accessed=6 * width * units + 4 * rows * width + 8 * rows * units,
            transcendentals=0,
        ),
        name="expert_backward",
    )(position, *chunks, swished, slope, w_gate, w_up, w_down)


def sum_kernel(pos_ref, own_ref, *refs):
    parts, out_ref = refs[:-1], refs[-1]
    size = own_ref.shape[0]
    total = jnp.zeros(own_ref.shape, F32)
    for part in parts:
        for start in range(0, part.shape[0], size):
            total = total + part[start : start + size, :].astype(F32)
    y_lo = pos_ref[1]
    out_ref[pl.ds(pl.multiple_of(y_lo * size, size), size), :] = own_ref[...]
    out_ref[pl.ds(pl.multiple_of((1 - y_lo) * size, size), size), :] = total.astype(BF16)


def sum_quarters(position, parts, own):
    rows, width = own.shape
    vmem = pl.BlockSpec(memory_space=pltpu.VMEM)
    return pl.pallas_call(
        sum_kernel,
        out_shape=jax.ShapeDtypeStruct((2 * rows, width), BF16),
        in_specs=[pl.BlockSpec(memory_space=pltpu.SMEM)] + [vmem] * (1 + len(parts)),
        out_specs=vmem,
        compiler_params=pltpu.CompilerParams(vmem_limit_bytes=VMEM_LIMIT),
        cost_estimate=pl.CostEstimate(
            flops=4 * rows * width, bytes_accessed=14 * rows * width, transcendentals=0
        ),
        name="sum_quarters",
    )(position, own, *parts)


def combine_kernel(slots, pos_ref, meta_ref, upstream_ref, *refs):
    outputs, grads, out_ref = refs[: 1 + SIDE], refs[1 + SIDE : 2 + 2 * SIDE], refs[-1]
    count, width = upstream_ref.shape
    meta = meta_ref[...]
    padded = 6 * slots
    target = slot_targets(pos_ref, lax.broadcasted_iota(jnp.int32, (count, padded), 1), slots).astype(F32)
    hit0 = (target == meta[:, 0:1]).astype(F32)
    hit1 = (target == meta[:, 1:2]).astype(F32)
    both = (hit0 + hit1).astype(BF16)
    hit0, hit1 = hit0.astype(BF16), hit1.astype(BF16)
    tile = column_tile(width)
    blank = jnp.zeros((slots, tile), BF16)
    dots0 = dots1 = jnp.zeros((count, 1), F32)

    def terms(parts, columns):
        return jnp.concatenate([ref[:, columns] for ref in parts] + [blank], axis=0)

    for start in range(0, width, tile):
        columns = slice(start, start + tile)
        out_terms = terms(outputs, columns)
        rows0 = jnp.dot(hit0, out_terms, preferred_element_type=F32)
        rows1 = jnp.dot(hit1, out_terms, preferred_element_type=F32)
        out_ref[:, columns] = (meta[:, 2:3] * rows0 + meta[:, 3:4] * rows1).astype(BF16)
        upstream = upstream_ref[:, columns].astype(F32)
        dots0 = dots0 + jnp.sum(upstream * rows0, axis=1, keepdims=True)
        dots1 = dots1 + jnp.sum(upstream * rows1, axis=1, keepdims=True)
        summed = jnp.dot(both, terms(grads, columns), preferred_element_type=F32)
        out_ref[:, width + start : width + start + tile] = summed.astype(BF16)
    lane = lax.broadcasted_iota(jnp.int32, (count, 128), 1)
    high0, high1 = dots0.astype(BF16).astype(F32), dots1.astype(BF16).astype(F32)
    extra = jnp.where(lane == 0, high0, 0.0)
    extra = jnp.where(lane == 1, dots0 - high0, extra)
    extra = jnp.where(lane == 2, high1, extra)
    extra = jnp.where(lane == 3, dots1 - high1, extra)
    out_ref[:, 2 * width :] = extra.astype(BF16)


def combine(position, meta, upstream, outputs, grads, slots):
    count, width = upstream.shape
    vmem = pl.BlockSpec(memory_space=pltpu.VMEM)
    return pl.pallas_call(
        functools.partial(combine_kernel, slots),
        out_shape=jax.ShapeDtypeStruct((count, 2 * width + 128), BF16),
        in_specs=[pl.BlockSpec(memory_space=pltpu.SMEM)] + [vmem] * (4 + 2 * SIDE),
        out_specs=vmem,
        compiler_params=pltpu.CompilerParams(vmem_limit_bytes=VMEM_LIMIT),
        cost_estimate=pl.CostEstimate(
            flops=6 * count * 6 * slots * width, bytes_accessed=20 * slots * width + 6 * count * width, transcendentals=0
        ),
        name="combine",
    )(position, meta, upstream, *outputs, *grads)


def finish_kernel(slots, pos_ref, meta_ref, router_ref, parts_ref, layer_ref, rows_ref):
    share = meta_ref.shape[0]
    width = layer_ref.shape[1]
    total = parts_ref[0:share, :].astype(F32)
    for k in range(1, parts_ref.shape[0] // share):
        total = total + parts_ref[k * share : (k + 1) * share, :].astype(F32)
    layer_ref[...] = total[:, :width].astype(BF16)
    grads = total[:, width : 2 * width]
    extra = total[:, 2 * width :]
    d_gap = (extra[:, 0:1] + extra[:, 1:2]) - (extra[:, 2:3] + extra[:, 3:4])
    meta = meta_ref[...]
    d_left = meta[:, 2:3] * meta[:, 3:4] * d_gap
    d_left = d_left.astype(BF16).astype(F32)
    chosen = meta.astype(jnp.int32) // slots
    router = router_ref[...].astype(F32)
    for e in range(router.shape[0]):
        sign = (chosen[:, 0:1] == e).astype(F32) - (chosen[:, 1:2] == e).astype(F32)
        grads = grads + (sign * d_left) * router[e : e + 1, :]
    rows_ref[...] = grads.astype(BF16)


def finish(position, meta, router, parts, share, slots):
    count, width = parts.shape[0], router.shape[1]
    whole = lambda *shape: pl.BlockSpec(shape, lambda i, pos: (0,) * len(shape))
    return pl.pallas_call(
        functools.partial(finish_kernel, slots),
        out_shape=[jax.ShapeDtypeStruct((share, width), BF16)] * 2,
        grid_spec=pltpu.PrefetchScalarGridSpec(
            num_scalar_prefetch=1,
            grid=(1,),
            in_specs=[
                pl.BlockSpec((share, meta.shape[1]), lambda i, pos: (pos[4], 0)),
                whole(*router.shape),
                whole(*parts.shape),
            ],
            out_specs=[whole(share, width)] * 2,
        ),
        compiler_params=pltpu.CompilerParams(vmem_limit_bytes=VMEM_LIMIT),
        cost_estimate=pl.CostEstimate(flops=30 * count * width, bytes_accessed=5 * count * width, transcendentals=0),
        name="finish",
    )(position, meta, router, parts)


def along(axis, sign, chunks):
    return [chunk if by == 0 else moved(chunk, axis, sign * by) for chunk, by in zip(chunks, STEPS)]


def halves(position, head, slots):
    y_lo = position[1]
    return [lax.dynamic_slice_in_dim(head, half * slots, slots, 0) for half in (y_lo, 1 - y_lo)]


def per_device(
    tokens_in, cotangent_in, expert_ids, router_weight, gate_weight, up_weight, down_weight
):
    swap = [(0, 1), (1, 0)]
    arrived = lax.ppermute(tokens_in[0], "pipe", swap)
    upstream = lax.ppermute(cotangent_in[0], "pipe", swap)
    routes = expert_ids[0].T
    router = router_weight[0].T
    w_gate = gate_weight[0, 0]
    w_up = up_weight[0, 0]
    w_down = down_weight[0, 0]
    count = arrived.shape[0]
    n_etp = lax.axis_size("etp")
    slots = 4 * count // lax.axis_size("expert")
    share = count // n_etp
    group = lax.axis_index("expert")
    part = lax.axis_index("etp")
    position = jnp.stack([group, group // SIDE, group % SIDE, part % SIDE, part]).astype(jnp.int32)
    meta, rows_head, *rows = dispatch_rows(position, routes, arrived, router, slots)
    rows_head = exchange(rows_head, "expert")
    *rows, rows_far = [rows[by] for by in STEPS]
    rows = along("expert", 1, rows)
    cot_head, *cot = dispatch_cot(position, meta, upstream, slots)
    rows_head, rows, cot_head = lax.optimization_barrier((rows_head, rows, cot_head))
    own, quarter = halves(position, rows_head, slots)
    quarters = along("etp", 1, [quarter] * SIDE)
    rows_far = moved(rows_far, "expert", STEPS[-1])
    cot_head = exchange(cot_head, "expert")
    rows_far, quarters, cot_head, cot = lax.optimization_barrier((rows_far, quarters, cot_head, cot))
    chunks = (*rows, rows_far, own, *quarters)
    own, quarter = halves(position, cot_head, slots)
    quarters = exchange(jnp.broadcast_to(quarter[None], (SIDE, *quarter.shape)).reshape(SIDE * slots, -1), "etp", low=True)
    cot = along("expert", 1, [cot[by] for by in STEPS])
    *out, own_out, out_quarters, swished, slope = forward(position, chunks, w_gate, w_up, w_down, slots)
    out_quarters = exchange(out_quarters, "etp", low=True)
    out = along("expert", -1, out)
    grad = backward(position, (*cot, own, quarters), swished, slope, w_gate, w_up, w_down, slots)
    out_quarters, out, grad = lax.optimization_barrier((out_quarters, out, grad))
    grad, own_grad, grad_quarters = grad[:SIDE], grad[SIDE], grad[1 + SIDE :]
    grad_quarters = along("etp", -1, grad_quarters)
    *grad, grad_far = grad
    grad = along("expert", -1, grad)
    out_head = exchange(sum_quarters(position, [out_quarters], own_out), "expert")
    grad_quarters, grad, out_head, grad_far = lax.optimization_barrier((grad_quarters, grad, out_head, grad_far))
    grad_head = exchange(sum_quarters(position, grad_quarters, own_grad), "expert")
    grad = [*grad, moved(grad_far, "expert", -STEPS[-1])]
    in_order = lambda head, chunks: [head] + [chunks[STEPS.index(by)] for by in range(SIDE)]
    parts = exchange(combine(position, meta, upstream, in_order(out_head, out), in_order(grad_head, grad), slots), "etp")
    layer_rows, grad_rows = finish(position, meta, router, parts, share, slots)
    return (layer_rows[None], grad_rows[None])


def solution(mesh):
    return jax.shard_map(
        per_device,
        mesh=mesh,
        in_specs=(
            P("pipe", "expert", None),
            P("pipe", "expert", None),
            P("pipe", None, None),
            P("pipe", None, None),
            P("pipe", "expert", None, "etp"),
            P("pipe", "expert", None, "etp"),
            P("pipe", "expert", "etp", None),
        ),
        out_specs=(P("pipe", ("expert", "etp"), None), P("pipe", ("expert", "etp"), None)),
        check_vma=False,
    )
```

```python
import functools

import jax
import jax.numpy as jnp
from jax import lax
from jax.experimental import pallas as pl
from jax.experimental.pallas import tpu as pltpu
from jax.sharding import PartitionSpec as P

F32 = jnp.float32
BF16 = jnp.bfloat16
SIDE = 4
STEPS = (0, 1, SIDE - 1, 2)
FORWARD_TILES = (256, 1024)
BACKWARD_TILES = (512, 512)
AHEAD = 2
VMEM_LIMIT = 56 * 1024 * 1024


def moved(x, axis, by):
    pairs = [(hi * SIDE + lo, hi * SIDE + (lo + by) % SIDE) for hi in range(2) for lo in range(SIDE)]
    return lax.ppermute(x, axis, pairs)


def exchange(x, axis, low=False):
    size = lax.axis_size(axis)
    groups = [list(range(start, start + SIDE)) for start in range(0, size, SIDE)] if low else None
    parts = SIDE if low else size
    blocks = x.reshape(parts, x.shape[0] // parts, x.shape[1])
    return lax.all_to_all(blocks, axis, 0, 0, axis_index_groups=groups).reshape(x.shape)


def column_tile(width):
    return 512 if width % 512 == 0 else width


def slot_targets(pos_ref, row, slots):
    y_lo, x, z = pos_ref[1], pos_ref[2], pos_ref[3]
    quarter = slots // SIDE
    head = 2 * SIDE * quarter
    expert = row // quarter
    first = expert * slots + jnp.where(expert // SIDE == y_lo, 0, z * quarter) + row % quarter
    rest = row - head
    more = slots - quarter
    second = (y_lo * SIDE + (x + rest // more) % SIDE) * slots + quarter + rest % more
    target = jnp.where(row < head, first, second)
    return jnp.where(row < head + SIDE * more, target, -1)


def slot_hits(slots, pos_ref, plan):
    count = plan.shape[0]
    total = 2 * slots + SIDE * (slots - slots // SIDE)
    flat = plan.T
    target = slot_targets(pos_ref, lax.broadcasted_iota(jnp.int32, (total, count), 0), slots).astype(F32)
    return (target == flat[0:1, :]).astype(F32), (target == flat[1:2, :]).astype(F32)


def plan_kernel(slots, pos_ref, ids_ref, plan_ref, hits_ref):
    count = plan_ref.shape[0]
    ids = ids_ref[:, pl.ds(pl.multiple_of(pos_ref[0] * count, count), count)].astype(F32)
    ids = jnp.concatenate([ids, jnp.zeros((count - 2, count), F32)], axis=0).T.astype(jnp.int32)
    first, second = ids[:, 0:1], ids[:, 1:2]
    lane = lax.broadcasted_iota(jnp.int32, (count, count), 1)
    row = lax.broadcasted_iota(jnp.int32, (count, count), 0)
    pick0 = (lane == first).astype(F32)
    pick1 = (lane == second).astype(F32)
    below = (row > lane).astype(F32).astype(BF16)
    before = jnp.dot(below, (pick0 + pick1).astype(BF16), preferred_element_type=F32)
    slot0 = first.astype(F32) * slots + jnp.sum(before * pick0, axis=1, keepdims=True)
    slot1 = second.astype(F32) * slots + jnp.sum(before * pick1, axis=1, keepdims=True)
    plan = jnp.where(lane == 0, slot0, jnp.where(lane == 1, slot1, 0.0))
    plan_ref[...] = plan
    hit0, hit1 = slot_hits(slots, pos_ref, plan)
    hits_ref[...] = (hit0 + hit1).astype(BF16)


def plan_slots(position, routes, count, slots):
    vmem = pl.BlockSpec(memory_space=pltpu.VMEM)
    total = 2 * slots + SIDE * (slots - slots // SIDE)
    return pl.pallas_call(
        functools.partial(plan_kernel, slots),
        out_shape=[jax.ShapeDtypeStruct((count, count), F32), jax.ShapeDtypeStruct((total, count), BF16)],
        in_specs=[pl.BlockSpec(memory_space=pltpu.SMEM), vmem],
        out_specs=[vmem] * 2,
        compiler_params=pltpu.CompilerParams(vmem_limit_bytes=VMEM_LIMIT),
        cost_estimate=pl.CostEstimate(flops=2 * count**3, bytes_accessed=8 * total * count, transcendentals=0),
        name="plan_slots",
    )(position, routes)


def write_rows(hits, scale, source_ref, refs):
    width = source_ref.shape[1]
    tile = column_tile(width)
    for start in range(0, width, tile):
        columns = slice(start, start + tile)
        rows = jnp.dot(hits, source_ref[:, columns], preferred_element_type=F32)
        if scale is not None:
            rows = scale * rows
        write_chunks(rows.astype(BF16), [ref.at[:, columns] for ref in refs])


def rows_kernel(hits_ref, arrived_ref, *refs):
    write_rows(hits_ref[...], None, arrived_ref, refs)


def cot_kernel(slots, pos_ref, plan_ref, arrived_ref, upstream_ref, router_ref, meta_ref, *refs):
    plan = plan_ref[...]
    scores = transposed_dot(arrived_ref[...], router_ref[...])
    expert = lax.broadcasted_iota(jnp.int32, scores.shape, 1)
    chosen = plan.astype(jnp.int32) // slots
    left = jnp.sum(jnp.where(expert == chosen[:, 0:1], scores, 0.0), axis=1, keepdims=True)
    right = jnp.sum(jnp.where(expert == chosen[:, 1:2], scores, 0.0), axis=1, keepdims=True)
    weight0 = 1.0 / (1.0 + jnp.exp(right - left))
    weight1 = 1.0 / (1.0 + jnp.exp(left - right))
    lane = lax.broadcasted_iota(jnp.int32, plan.shape, 1)
    meta = jnp.where(lane == 2, weight0, jnp.where(lane == 3, weight1, plan))
    meta_ref[...] = meta
    hit0, hit1 = slot_hits(slots, pos_ref, plan)
    flat = meta.T
    scale = jnp.sum(hit0 * flat[2:3, :] + hit1 * flat[3:4, :], axis=1, keepdims=True)
    write_rows((hit0 + hit1).astype(BF16), scale, upstream_ref, refs)


def dispatch_shapes(slots, width):
    return [jax.ShapeDtypeStruct((2 * slots, width), BF16)] + [
        jax.ShapeDtypeStruct((slots - slots // SIDE, width), BF16)
    ] * SIDE


def dispatch_rows(hits, arrived, slots):
    count, width = arrived.shape
    vmem = pl.BlockSpec(memory_space=pltpu.VMEM)
    outs = dispatch_shapes(slots, width)
    return pl.pallas_call(
        rows_kernel,
        out_shape=outs,
        in_specs=[vmem] * 2,
        out_specs=[vmem] * len(outs),
        compiler_params=pltpu.CompilerParams(vmem_limit_bytes=VMEM_LIMIT),
        cost_estimate=pl.CostEstimate(
            flops=2 * 5 * slots * count * width, bytes_accessed=8 * count * width, transcendentals=0
        ),
        name="dispatch_rows",
    )(hits, arrived)


def dispatch_cot(position, plan, arrived, upstream, router, slots):
    count, width = upstream.shape
    vmem = pl.BlockSpec(memory_space=pltpu.VMEM)
    outs = [jax.ShapeDtypeStruct(plan.shape, F32)] + dispatch_shapes(slots, width)
    return pl.pallas_call(
        functools.partial(cot_kernel, slots),
        out_shape=outs,
        in_specs=[pl.BlockSpec(memory_space=pltpu.SMEM)] + [vmem] * 4,
        out_specs=[vmem] * len(outs),
        compiler_params=pltpu.CompilerParams(vmem_limit_bytes=VMEM_LIMIT),
        cost_estimate=pl.CostEstimate(
            flops=2 * 5 * slots * count * width, bytes_accessed=10 * count * width, transcendentals=0
        ),
        name="dispatch_cot",
    )(position, plan, arrived, upstream, router)


def chunk_places(pos_ref, slots, apart):
    more = slots - slots // SIDE
    places = [(k * more, more) for k in range(SIDE)] + [(SIDE * more, slots)]
    base = SIDE * more + slots
    if not apart:
        return places + [(base, SIDE * slots)]
    z = pos_ref[3]
    return places + [(pl.multiple_of(base + lax.rem(z + SIDE - by, SIDE) * slots, slots), slots) for by in STEPS]


def chunk_shapes(slots, width, apart):
    sizes = [slots - slots // SIDE] * SIDE + [slots] + ([slots] * SIDE if apart else [SIDE * slots])
    return [jax.ShapeDtypeStruct((size, width), BF16) for size in sizes]


def row_copies(places, refs, rows_v, sems):
    return [
        pltpu.make_async_copy(ref, rows_v.at[pl.ds(start, size)], sems.at[k])
        for k, ((start, size), ref) in enumerate(zip(places, refs))
    ]


def result_copies(places, rows_v, columns, refs, sems):
    return [
        pltpu.make_async_copy(rows_v.at[pl.ds(start, size), columns], ref.at[:, columns], sems.at[k])
        for k, ((start, size), ref) in enumerate(zip(places, refs))
    ]


def tiles(extent, size):
    size = size if extent % size == 0 else extent
    return [pl.ds(start, size) for start in range(0, extent, size)]


def begin(copies):
    for copy in copies:
        copy.start()


def finish_copies(copies):
    for copy in copies:
        copy.wait()


def write_chunks(out, refs):
    start = 0
    for ref in refs:
        size = ref.shape[0]
        ref[...] = out[start : start + size]
        start += size


def forward_kernel(slots, pos_ref, *refs):
    places_in, places_out = chunk_places(pos_ref, slots, True), chunk_places(pos_ref, slots, False)
    chunks, refs = refs[: len(places_in)], refs[len(places_in) :]
    (gate, up, down), refs = refs[:3], refs[3:]
    outs, refs = refs[: len(places_out)], refs[len(places_out) :]
    (swished, slope), refs = refs[:2], refs[2:]
    rows_v, gate_v, up_v, down_v, gate_pre, up_pre, swished_v, slope_v, hidden_v, out_v, *sems = refs
    row_sem, gate_sem, up_sem, down_sem, swished_sem, slope_sem, out_sem = sems
    units, width = down.shape
    unit_tiles, column_tiles = tiles(units, FORWARD_TILES[0]), tiles(width, FORWARD_TILES[1])
    loads = []
    for k, part in enumerate(unit_tiles):
        loads.append(
            [
                pltpu.make_async_copy(gate.at[:, part], gate_v.at[:, part], gate_sem.at[k]),
                pltpu.make_async_copy(up.at[:, part], up_v.at[:, part], up_sem.at[k]),
            ]
        )
    for k, part in enumerate(column_tiles):
        loads.append([pltpu.make_async_copy(down.at[:, part], down_v.at[:, part], down_sem.at[k])])
    saves = []

    def activate(k):
        part = unit_tiles[k]
        gates, ups = gate_pre[k % 2], up_pre[k % 2]
        sigmoid_part = jax.nn.sigmoid(gates)
        swish = gates * sigmoid_part
        swished_v[:, part] = swish
        slope_v[:, part] = ups * (sigmoid_part * (1.0 + gates * (1.0 - sigmoid_part)))
        hidden_v[:, part] = (swish * ups).astype(BF16)

    def save(k):
        part = unit_tiles[k]
        copies = [
            pltpu.make_async_copy(swished_v.at[:, part], swished.at[:, part], swished_sem.at[k]),
            pltpu.make_async_copy(slope_v.at[:, part], slope.at[:, part], slope_sem.at[k]),
        ]
        begin(copies)
        saves.extend(copies)

    rows = row_copies(places_in, chunks, rows_v, row_sem)
    begin(rows)
    for k in range(AHEAD):
        begin(loads[k])
    finish_copies(rows)
    for k, part in enumerate(unit_tiles):
        finish_copies(loads[k])
        if k + AHEAD < len(loads):
            begin(loads[k + AHEAD])
        gate_pre[k % 2] = jnp.dot(rows_v[...], gate_v[:, part], preferred_element_type=F32)
        up_pre[k % 2] = jnp.dot(rows_v[...], up_v[:, part], preferred_element_type=F32)
        if k > 0:
            activate(k - 1)
            save(k - 1)
    activate(len(unit_tiles) - 1)
    save(len(unit_tiles) - 1)
    for k, part in enumerate(column_tiles):
        at = len(unit_tiles) + k
        finish_copies(loads[at])
        if at + AHEAD < len(loads):
            begin(loads[at + AHEAD])
        out_v[:, part] = jnp.dot(hidden_v[...], down_v[:, part], preferred_element_type=F32).astype(BF16)
        copies = result_copies(places_out, out_v, part, outs, out_sem.at[k])
        begin(copies)
        saves.extend(copies)
    finish_copies(saves)


def forward(position, chunks, w_gate, w_up, w_down, slots):
    width, units = w_gate.shape
    outs = chunk_shapes(slots, width, False)
    rows = sum(out.shape[0] for out in outs)
    unit_tiles, column_tiles = tiles(units, FORWARD_TILES[0]), tiles(width, FORWARD_TILES[1])
    unit_tile = unit_tiles[0].size
    anywhere = pl.BlockSpec(memory_space=pl.ANY)
    dma = pltpu.SemaphoreType.DMA
    results = pl.pallas_call(
        functools.partial(forward_kernel, slots),
        out_shape=outs + [jax.ShapeDtypeStruct((rows, units), F32)] * 2,
        in_specs=[pl.BlockSpec(memory_space=pltpu.SMEM)] + [anywhere] * (len(chunks) + 3),
        out_specs=[anywhere] * (len(outs) + 2),
        scratch_shapes=[
            pltpu.VMEM((rows, width), BF16),
            pltpu.VMEM((width, units), BF16),
            pltpu.VMEM((width, units), BF16),
            pltpu.VMEM((units, width), BF16),
            pltpu.VMEM((2, rows, unit_tile), F32),
            pltpu.VMEM((2, rows, unit_tile), F32),
            pltpu.VMEM((rows, units), F32),
            pltpu.VMEM((rows, units), F32),
            pltpu.VMEM((rows, units), BF16),
            pltpu.VMEM((rows, width), BF16),
            dma((len(chunks),)),
            dma((len(unit_tiles),)),
            dma((len(unit_tiles),)),
            dma((len(column_tiles),)),
            dma((len(unit_tiles),)),
            dma((len(unit_tiles),)),
            dma((len(column_tiles), len(outs))),
        ],
        compiler_params=pltpu.CompilerParams(vmem_limit_bytes=VMEM_LIMIT),
        cost_estimate=pl.CostEstimate(
            flops=6 * rows * width * units,
            bytes_accessed=6 * width * units + 4 * rows * width + 8 * rows * units,
            transcendentals=rows * units,
        ),
        name="expert_forward",
    )(position, *chunks, w_gate, w_up, w_down)
    return results


def transposed_dot(a, b):
    return lax.dot_general(a, b, (((1,), (1,)), ((), ())), preferred_element_type=F32)


def backward_kernel(slots, pos_ref, *refs):
    places_in, places_out = chunk_places(pos_ref, slots, False), chunk_places(pos_ref, slots, True)
    chunks, refs = refs[: len(places_in)], refs[len(places_in) :]
    (swished, slope, gate, up, down), refs = refs[:5], refs[5:]
    outs, refs = refs[: len(places_out)], refs[len(places_out) :]
    cot_v, gate_v, up_v, down_v, swished_v, slope_v, d_hidden, d_gate, d_up, out_v, *sems = refs
    row_sem, gate_sem, up_sem, down_sem, swished_sem, slope_sem, out_sem = sems
    units, width = down.shape
    unit_tiles, column_tiles = tiles(units, BACKWARD_TILES[0]), tiles(width, BACKWARD_TILES[1])
    loads = []
    for k, part in enumerate(unit_tiles):
        loads.append(
            [
                pltpu.make_async_copy(down.at[part], down_v.at[part], down_sem.at[k]),
                pltpu.make_async_copy(swished.at[:, part], swished_v.at[:, part], swished_sem.at[k]),
                pltpu.make_async_copy(slope.at[:, part], slope_v.at[:, part], slope_sem.at[k]),
            ]
        )
    for k, part in enumerate(column_tiles):
        loads.append(
            [
                pltpu.make_async_copy(gate.at[part], gate_v.at[part], gate_sem.at[k]),
                pltpu.make_async_copy(up.at[part], up_v.at[part], up_sem.at[k]),
            ]
        )
    saves = []

    def activate(k):
        part = unit_tiles[k]
        d_up[:, part] = (d_hidden[k % 2] * swished_v[:, part]).astype(BF16)
        d_gate[:, part] = (d_hidden[k % 2] * slope_v[:, part]).astype(BF16)

    rows = row_copies(places_in, chunks, cot_v, row_sem)
    begin(rows)
    for k in range(AHEAD):
        begin(loads[k])
    finish_copies(rows)
    for k, part in enumerate(unit_tiles):
        finish_copies(loads[k])
        if k + AHEAD < len(loads):
            begin(loads[k + AHEAD])
        d_hidden[k % 2] = transposed_dot(cot_v[...], down_v[part, :])
        if k > 0:
            activate(k - 1)
    activate(len(unit_tiles) - 1)
    for k, part in enumerate(column_tiles):
        at = len(unit_tiles) + k
        finish_copies(loads[at])
        if at + AHEAD < len(loads):
            begin(loads[at + AHEAD])
        out = transposed_dot(d_gate[...], gate_v[part, :]) + transposed_dot(d_up[...], up_v[part, :])
        out_v[:, part] = out.astype(BF16)
        copies = result_copies(places_out, out_v, part, outs, out_sem.at[k])
        begin(copies)
        saves.extend(copies)
    finish_copies(saves)


def backward(position, chunks, swished, slope, w_gate, w_up, w_down, slots):
    width, units = w_gate.shape
    outs = chunk_shapes(slots, width, True)
    rows = sum(out.shape[0] for out in outs)
    unit_tiles, column_tiles = tiles(units, BACKWARD_TILES[0]), tiles(width, BACKWARD_TILES[1])
    anywhere = pl.BlockSpec(memory_space=pl.ANY)
    dma = pltpu.SemaphoreType.DMA
    return pl.pallas_call(
        functools.partial(backward_kernel, slots),
        out_shape=outs,
        in_specs=[pl.BlockSpec(memory_space=pltpu.SMEM)] + [anywhere] * (len(chunks) + 5),
        out_specs=[anywhere] * len(outs),
        scratch_shapes=[
            pltpu.VMEM((rows, width), BF16),
            pltpu.VMEM((width, units), BF16),
            pltpu.VMEM((width, units), BF16),
            pltpu.VMEM((units, width), BF16),
            pltpu.VMEM((rows, units), F32),
            pltpu.VMEM((rows, units), F32),
            pltpu.VMEM((2, rows, unit_tiles[0].size), F32),
            pltpu.VMEM((rows, units), BF16),
            pltpu.VMEM((rows, units), BF16),
            pltpu.VMEM((rows, width), BF16),
            dma((len(chunks),)),
            dma((len(column_tiles),)),
            dma((len(column_tiles),)),
            dma((len(unit_tiles),)),
            dma((len(unit_tiles),)),
            dma((len(unit_tiles),)),
            dma((len(column_tiles), len(outs))),
        ],
        compiler_params=pltpu.CompilerParams(vmem_limit_bytes=VMEM_LIMIT),
        cost_estimate=pl.CostEstimate(
            flops=6 * rows * width * units,
            bytes_accessed=6 * width * units + 4 * rows * width + 8 * rows * units,
            transcendentals=0,
        ),
        name="expert_backward",
    )(position, *chunks, swished, slope, w_gate, w_up, w_down)


def sum_kernel(pos_ref, own_ref, *refs):
    parts, out_ref = refs[:-1], refs[-1]
    size = own_ref.shape[0]
    total = jnp.zeros(own_ref.shape, F32)
    for part in parts:
        for start in range(0, part.shape[0], size):
            total = total + part[start : start + size, :].astype(F32)
    y_lo = pos_ref[1]
    out_ref[pl.ds(pl.multiple_of(y_lo * size, size), size), :] = own_ref[...]
    out_ref[pl.ds(pl.multiple_of((1 - y_lo) * size, size), size), :] = total.astype(BF16)


def sum_quarters(position, parts, own):
    rows, width = own.shape
    vmem = pl.BlockSpec(memory_space=pltpu.VMEM)
    return pl.pallas_call(
        sum_kernel,
        out_shape=jax.ShapeDtypeStruct((2 * rows, width), BF16),
        in_specs=[pl.BlockSpec(memory_space=pltpu.SMEM)] + [vmem] * (1 + len(parts)),
        out_specs=vmem,
        compiler_params=pltpu.CompilerParams(vmem_limit_bytes=VMEM_LIMIT),
        cost_estimate=pl.CostEstimate(
            flops=4 * rows * width, bytes_accessed=14 * rows * width, transcendentals=0
        ),
        name="sum_quarters",
    )(position, own, *parts)


def combine_hits(slots, pos_ref, meta):
    count = meta.shape[0]
    target = slot_targets(pos_ref, lax.broadcasted_iota(jnp.int32, (count, 6 * slots), 1), slots).astype(F32)
    return (target == meta[:, 0:1]).astype(F32), (target == meta[:, 1:2]).astype(F32)


def returned_rows(refs, columns, blank):
    return jnp.concatenate([ref[:, columns] for ref in refs] + [jnp.zeros(blank, BF16)], axis=0)


def combine_out_kernel(slots, pos_ref, meta_ref, upstream_ref, *refs):
    returned, (out_ref, dots_ref) = refs[:-2], refs[-2:]
    count, width = upstream_ref.shape
    meta = meta_ref[...]
    hit0, hit1 = [hit.astype(BF16) for hit in combine_hits(slots, pos_ref, meta)]
    tile = column_tile(width)
    dots0 = dots1 = jnp.zeros((count, 1), F32)
    for start in range(0, width, tile):
        columns = slice(start, start + tile)
        terms = returned_rows(returned, columns, (slots, tile))
        rows0 = jnp.dot(hit0, terms, preferred_element_type=F32)
        rows1 = jnp.dot(hit1, terms, preferred_element_type=F32)
        out_ref[:, columns] = (meta[:, 2:3] * rows0 + meta[:, 3:4] * rows1).astype(BF16)
        upstream = upstream_ref[:, columns].astype(F32)
        dots0 = dots0 + jnp.sum(upstream * rows0, axis=1, keepdims=True)
        dots1 = dots1 + jnp.sum(upstream * rows1, axis=1, keepdims=True)
    lane = lax.broadcasted_iota(jnp.int32, dots_ref.shape, 1)
    high0, high1 = dots0.astype(BF16).astype(F32), dots1.astype(BF16).astype(F32)
    extra = jnp.where(lane == 0, high0, 0.0)
    extra = jnp.where(lane == 1, dots0 - high0, extra)
    extra = jnp.where(lane == 2, high1, extra)
    extra = jnp.where(lane == 3, dots1 - high1, extra)
    dots_ref[...] = extra.astype(BF16)


def combine_out(position, meta, upstream, returned, slots):
    count, width = upstream.shape
    vmem = pl.BlockSpec(memory_space=pltpu.VMEM)
    return pl.pallas_call(
        functools.partial(combine_out_kernel, slots),
        out_shape=[jax.ShapeDtypeStruct((count, size), BF16) for size in (width, 128)],
        in_specs=[pl.BlockSpec(memory_space=pltpu.SMEM)] + [vmem] * (3 + SIDE),
        out_specs=[vmem] * 2,
        compiler_params=pltpu.CompilerParams(vmem_limit_bytes=VMEM_LIMIT),
        cost_estimate=pl.CostEstimate(
            flops=4 * count * 6 * slots * width, bytes_accessed=10 * slots * width + 4 * count * width, transcendentals=0
        ),
        name="combine_out",
    )(position, meta, upstream, *returned)


def combine_grad_kernel(slots, pos_ref, meta_ref, out_terms_ref, dots_ref, *refs):
    returned, out_ref = refs[:-1], refs[-1]
    width = returned[0].shape[1]
    hit0, hit1 = combine_hits(slots, pos_ref, meta_ref[...])
    both = (hit0 + hit1).astype(BF16)
    tile = column_tile(width)
    for start in range(0, width, tile):
        columns = slice(start, start + tile)
        terms = returned_rows(returned, columns, (slots, tile))
        out_ref[:, columns] = out_terms_ref[:, columns]
        grads = jnp.dot(both, terms, preferred_element_type=F32)
        out_ref[:, width + start : width + start + tile] = grads.astype(BF16)
    out_ref[:, 2 * width :] = dots_ref[...]


def combine_grad(position, meta, out_terms, dots, returned, slots):
    count, width = out_terms.shape
    vmem = pl.BlockSpec(memory_space=pltpu.VMEM)
    return pl.pallas_call(
        functools.partial(combine_grad_kernel, slots),
        out_shape=jax.ShapeDtypeStruct((count, 2 * width + dots.shape[1]), BF16),
        in_specs=[pl.BlockSpec(memory_space=pltpu.SMEM)] + [vmem] * (4 + SIDE),
        out_specs=vmem,
        compiler_params=pltpu.CompilerParams(vmem_limit_bytes=VMEM_LIMIT),
        cost_estimate=pl.CostEstimate(
            flops=2 * count * 6 * slots * width, bytes_accessed=10 * slots * width + 6 * count * width, transcendentals=0
        ),
        name="combine_grad",
    )(position, meta, out_terms, dots, *returned)


def finish_kernel(slots, pos_ref, meta_ref, router_ref, parts_ref, layer_ref, rows_ref):
    share, width = layer_ref.shape
    sums = parts_ref[0:share, :].astype(F32)
    for k in range(1, parts_ref.shape[0] // share):
        sums = sums + parts_ref[k * share : (k + 1) * share, :].astype(F32)
    layer_ref[...] = sums[:, :width].astype(BF16)
    grads, extra = sums[:, width : 2 * width], sums[:, 2 * width :]
    d_gap = (extra[:, 0:1] + extra[:, 1:2]) - (extra[:, 2:3] + extra[:, 3:4])
    meta = meta_ref[pl.ds(pl.multiple_of(pos_ref[4] * share, share), share), :]
    d_left = meta[:, 2:3] * meta[:, 3:4] * d_gap
    d_left = d_left.astype(BF16).astype(F32)
    chosen = meta.astype(jnp.int32) // slots
    router = router_ref[...].astype(F32)
    for e in range(router.shape[0]):
        sign = (chosen[:, 0:1] == e).astype(F32) - (chosen[:, 1:2] == e).astype(F32)
        grads = grads + (sign * d_left) * router[e : e + 1, :]
    rows_ref[...] = grads.astype(BF16)


def finish(position, meta, router, parts, share, slots):
    width = router.shape[1]
    vmem = pl.BlockSpec(memory_space=pltpu.VMEM)
    return pl.pallas_call(
        functools.partial(finish_kernel, slots),
        out_shape=[jax.ShapeDtypeStruct((share, width), BF16)] * 2,
        in_specs=[pl.BlockSpec(memory_space=pltpu.SMEM)] + [vmem] * 3,
        out_specs=[vmem] * 2,
        compiler_params=pltpu.CompilerParams(vmem_limit_bytes=VMEM_LIMIT),
        cost_estimate=pl.CostEstimate(
            flops=30 * parts.shape[0] * width, bytes_accessed=5 * parts.shape[0] * width, transcendentals=0
        ),
        name="finish",
    )(position, meta, router, parts)


def along(axis, sign, chunks):
    return [chunk if by == 0 else moved(chunk, axis, sign * by) for chunk, by in zip(chunks, STEPS)]


def halves(position, head, slots):
    y_lo = position[1]
    return [lax.dynamic_slice_in_dim(head, half * slots, slots, 0) for half in (y_lo, 1 - y_lo)]


def per_device(
    tokens_in, cotangent_in, expert_ids, router_weight, gate_weight, up_weight, down_weight
):
    swap = [(0, 1), (1, 0)]
    arrived = lax.ppermute(tokens_in[0], "pipe", swap)
    upstream = lax.ppermute(cotangent_in[0], "pipe", swap)
    routes = expert_ids[0].T
    router = router_weight[0].T
    w_gate = gate_weight[0, 0]
    w_up = up_weight[0, 0]
    w_down = down_weight[0, 0]
    count = arrived.shape[0]
    slots = 4 * count // lax.axis_size("expert")
    group = lax.axis_index("expert")
    part = lax.axis_index("etp")
    position = jnp.stack([group, group // SIDE, group % SIDE, part % SIDE, part]).astype(jnp.int32)
    plan, hits = plan_slots(position, routes, count, slots)
    rows_head, *rows = dispatch_rows(hits, arrived, slots)
    rows_head = exchange(rows_head, "expert")
    *rows, rows_far = [rows[by] for by in STEPS]
    rows = along("expert", 1, rows)
    meta, cot_head, *cot = dispatch_cot(position, plan, arrived, upstream, router, slots)
    rows_head, rows = lax.optimization_barrier((rows_head, rows))
    own, quarter = halves(position, rows_head, slots)
    quarters = along("etp", 1, [quarter] * SIDE)
    rows_far = moved(rows_far, "expert", STEPS[-1])
    cot_head = exchange(cot_head, "expert")
    rows_far, quarters, cot_head, cot = lax.optimization_barrier((rows_far, quarters, cot_head, cot))
    chunks = (*rows, rows_far, own, *quarters)
    own, quarter = halves(position, cot_head, slots)
    quarters = exchange(jnp.broadcast_to(quarter[None], (SIDE, *quarter.shape)).reshape(SIDE * slots, -1), "etp", low=True)
    cot = along("expert", 1, [cot[by] for by in STEPS])
    *out, own_out, out_quarters, swished, slope = forward(position, chunks, w_gate, w_up, w_down, slots)
    out_quarters = exchange(out_quarters, "etp", low=True)
    out = along("expert", -1, out)
    grad = backward(position, (*cot, own, quarters), swished, slope, w_gate, w_up, w_down, slots)
    out_quarters, out, grad = lax.optimization_barrier((out_quarters, out, grad))
    grad, own_grad, grad_quarters = grad[:SIDE], grad[SIDE], grad[1 + SIDE :]
    grad_quarters = along("etp", -1, grad_quarters)
    grad = along("expert", -1, grad)
    in_order = lambda head, chunks: [head] + [chunks[STEPS.index(by)] for by in range(SIDE)]
    out_head = exchange(sum_quarters(position, [out_quarters], own_out), "expert")
    grad_quarters, grad, out_head = lax.optimization_barrier((grad_quarters, grad, out_head))
    out_terms, dots = combine_out(position, meta, upstream, in_order(out_head, out), slots)
    grad_head = exchange(sum_quarters(position, grad_quarters, own_grad), "expert")
    terms = combine_grad(position, meta, out_terms, dots, in_order(grad_head, grad), slots)
    share = count // lax.axis_size("etp")
    layer_rows, grad_rows = finish(position, meta, router, exchange(terms, "etp"), share, slots)
    return (layer_rows[None], grad_rows[None])


def solution(mesh):
    return jax.shard_map(
        per_device,
        mesh=mesh,
        in_specs=(
            P("pipe", "expert", None),
            P("pipe", "expert", None),
            P("pipe", None, None),
            P("pipe", None, None),
            P("pipe", "expert", None, "etp"),
            P("pipe", "expert", None, "etp"),
            P("pipe", "expert", "etp", None),
        ),
        out_specs=(P("pipe", ("expert", "etp"), None), P("pipe", ("expert", "etp"), None)),
        check_vma=False,
    )
```

```python
import functools

import jax
import jax.numpy as jnp
from jax import lax
from jax.experimental import pallas as pl
from jax.experimental.pallas import tpu as pltpu
from jax.sharding import PartitionSpec as P

F32 = jnp.float32
BF16 = jnp.bfloat16
SIDE = 4
STEPS = (0, 1, SIDE - 1, 2)
FORWARD_TILES = (256, 1024)
BACKWARD_TILES = (512, 1024)
AHEAD = 2
VMEM_LIMIT = 56 * 1024 * 1024


def moved(x, axis, by):
    pairs = [(hi * SIDE + lo, hi * SIDE + (lo + by) % SIDE) for hi in range(2) for lo in range(SIDE)]
    return lax.ppermute(x, axis, pairs)


def exchange(x, axis, low=False):
    size = lax.axis_size(axis)
    groups = [list(range(start, start + SIDE)) for start in range(0, size, SIDE)] if low else None
    parts = SIDE if low else size
    blocks = x.reshape(parts, x.shape[0] // parts, x.shape[1])
    return lax.all_to_all(blocks, axis, 0, 0, axis_index_groups=groups).reshape(x.shape)


def column_tile(width):
    return 512 if width % 512 == 0 else width


def slot_targets(pos_ref, row, slots):
    y_lo, x, z = pos_ref[1], pos_ref[2], pos_ref[3]
    quarter = slots // SIDE
    head = 2 * SIDE * quarter
    expert = row // quarter
    first = expert * slots + jnp.where(expert // SIDE == y_lo, 0, z * quarter) + row % quarter
    rest = row - head
    more = slots - quarter
    second = (y_lo * SIDE + (x + rest // more) % SIDE) * slots + quarter + rest % more
    target = jnp.where(row < head, first, second)
    return jnp.where(row < head + SIDE * more, target, -1)


def slot_hits(slots, pos_ref, plan):
    count = plan.shape[0]
    total = 2 * slots + SIDE * (slots - slots // SIDE)
    flat = plan.T
    target = slot_targets(pos_ref, lax.broadcasted_iota(jnp.int32, (total, count), 0), slots).astype(F32)
    return (target == flat[0:1, :]).astype(F32), (target == flat[1:2, :]).astype(F32)


def plan_kernel(slots, pos_ref, ids_ref, plan_ref, hits_ref):
    count = plan_ref.shape[0]
    ids = ids_ref[:, pl.ds(pl.multiple_of(pos_ref[0] * count, count), count)].astype(F32)
    ids = jnp.concatenate([ids, jnp.zeros((count - 2, count), F32)], axis=0).T.astype(jnp.int32)
    first, second = ids[:, 0:1], ids[:, 1:2]
    lane = lax.broadcasted_iota(jnp.int32, (count, count), 1)
    row = lax.broadcasted_iota(jnp.int32, (count, count), 0)
    pick0 = (lane == first).astype(F32)
    pick1 = (lane == second).astype(F32)
    below = (row > lane).astype(F32).astype(BF16)
    before = jnp.dot(below, (pick0 + pick1).astype(BF16), preferred_element_type=F32)
    slot0 = first.astype(F32) * slots + jnp.sum(before * pick0, axis=1, keepdims=True)
    slot1 = second.astype(F32) * slots + jnp.sum(before * pick1, axis=1, keepdims=True)
    plan = jnp.where(lane == 0, slot0, jnp.where(lane == 1, slot1, 0.0))
    plan_ref[...] = plan
    hit0, hit1 = slot_hits(slots, pos_ref, plan)
    hits_ref[...] = (hit0 + hit1).astype(BF16)


def plan_slots(position, routes, count, slots):
    vmem = pl.BlockSpec(memory_space=pltpu.VMEM)
    total = 2 * slots + SIDE * (slots - slots // SIDE)
    return pl.pallas_call(
        functools.partial(plan_kernel, slots),
        out_shape=[jax.ShapeDtypeStruct((count, count), F32), jax.ShapeDtypeStruct((total, count), BF16)],
        in_specs=[pl.BlockSpec(memory_space=pltpu.SMEM), vmem],
        out_specs=[vmem] * 2,
        compiler_params=pltpu.CompilerParams(vmem_limit_bytes=VMEM_LIMIT),
        cost_estimate=pl.CostEstimate(flops=2 * count**3, bytes_accessed=8 * total * count, transcendentals=0),
        name="plan_slots",
    )(position, routes)


def write_rows(hits, scale, source_ref, refs):
    width = source_ref.shape[1]
    tile = column_tile(width)
    for start in range(0, width, tile):
        columns = slice(start, start + tile)
        rows = jnp.dot(hits, source_ref[:, columns], preferred_element_type=F32)
        if scale is not None:
            rows = scale * rows
        write_chunks(rows.astype(BF16), [ref.at[:, columns] for ref in refs])


def rows_kernel(hits_ref, arrived_ref, *refs):
    write_rows(hits_ref[...], None, arrived_ref, refs)


def cot_kernel(slots, pos_ref, plan_ref, arrived_ref, upstream_ref, router_ref, meta_ref, *refs):
    plan = plan_ref[...]
    scores = transposed_dot(arrived_ref[...], router_ref[...])
    expert = lax.broadcasted_iota(jnp.int32, scores.shape, 1)
    chosen = plan.astype(jnp.int32) // slots
    left = jnp.sum(jnp.where(expert == chosen[:, 0:1], scores, 0.0), axis=1, keepdims=True)
    right = jnp.sum(jnp.where(expert == chosen[:, 1:2], scores, 0.0), axis=1, keepdims=True)
    weight0 = 1.0 / (1.0 + jnp.exp(right - left))
    weight1 = 1.0 / (1.0 + jnp.exp(left - right))
    lane = lax.broadcasted_iota(jnp.int32, plan.shape, 1)
    meta = jnp.where(lane == 2, weight0, jnp.where(lane == 3, weight1, plan))
    meta_ref[...] = meta
    hit0, hit1 = slot_hits(slots, pos_ref, plan)
    flat = meta.T
    scale = jnp.sum(hit0 * flat[2:3, :] + hit1 * flat[3:4, :], axis=1, keepdims=True)
    write_rows((hit0 + hit1).astype(BF16), scale, upstream_ref, refs)


def dispatch_shapes(slots, width):
    return [jax.ShapeDtypeStruct((2 * slots, width), BF16)] + [
        jax.ShapeDtypeStruct((slots - slots // SIDE, width), BF16)
    ] * SIDE


def dispatch_rows(hits, arrived, slots):
    count, width = arrived.shape
    vmem = pl.BlockSpec(memory_space=pltpu.VMEM)
    outs = dispatch_shapes(slots, width)
    return pl.pallas_call(
        rows_kernel,
        out_shape=outs,
        in_specs=[vmem] * 2,
        out_specs=[vmem] * len(outs),
        compiler_params=pltpu.CompilerParams(vmem_limit_bytes=VMEM_LIMIT),
        cost_estimate=pl.CostEstimate(
            flops=2 * 5 * slots * count * width, bytes_accessed=8 * count * width, transcendentals=0
        ),
        name="dispatch_rows",
    )(hits, arrived)


def dispatch_cot(position, plan, arrived, upstream, router, slots):
    count, width = upstream.shape
    vmem = pl.BlockSpec(memory_space=pltpu.VMEM)
    outs = [jax.ShapeDtypeStruct(plan.shape, F32)] + dispatch_shapes(slots, width)
    return pl.pallas_call(
        functools.partial(cot_kernel, slots),
        out_shape=outs,
        in_specs=[pl.BlockSpec(memory_space=pltpu.SMEM)] + [vmem] * 4,
        out_specs=[vmem] * len(outs),
        compiler_params=pltpu.CompilerParams(vmem_limit_bytes=VMEM_LIMIT),
        cost_estimate=pl.CostEstimate(
            flops=2 * 5 * slots * count * width, bytes_accessed=10 * count * width, transcendentals=0
        ),
        name="dispatch_cot",
    )(position, plan, arrived, upstream, router)


def chunk_places(pos_ref, slots, apart):
    more = slots - slots // SIDE
    places = [(k * more, more) for k in range(SIDE)] + [(SIDE * more, slots)]
    base = SIDE * more + slots
    if not apart:
        return places + [(base, SIDE * slots)]
    z = pos_ref[3]
    return places + [(pl.multiple_of(base + lax.rem(z + SIDE - by, SIDE) * slots, slots), slots) for by in STEPS]


def chunk_shapes(slots, width, apart):
    sizes = [slots - slots // SIDE] * SIDE + [slots] + ([slots] * SIDE if apart else [SIDE * slots])
    return [jax.ShapeDtypeStruct((size, width), BF16) for size in sizes]


def row_copies(places, refs, rows_v, sems):
    return [
        pltpu.make_async_copy(ref, rows_v.at[pl.ds(start, size)], sems.at[k])
        for k, ((start, size), ref) in enumerate(zip(places, refs))
    ]


def result_copies(places, rows_v, columns, refs, sems):
    return [
        pltpu.make_async_copy(rows_v.at[pl.ds(start, size), columns], ref.at[:, columns], sems.at[k])
        for k, ((start, size), ref) in enumerate(zip(places, refs))
    ]


def tiles(extent, size):
    size = size if extent % size == 0 else extent
    return [pl.ds(start, size) for start in range(0, extent, size)]


def begin(copies):
    for copy in copies:
        copy.start()


def finish_copies(copies):
    for copy in copies:
        copy.wait()


def write_chunks(out, refs):
    start = 0
    for ref in refs:
        size = ref.shape[0]
        ref[...] = out[start : start + size]
        start += size


def forward_kernel(slots, pos_ref, *refs):
    places_in, places_out = chunk_places(pos_ref, slots, True), chunk_places(pos_ref, slots, False)
    chunks, refs = refs[: len(places_in)], refs[len(places_in) :]
    (gate, up, down), refs = refs[:3], refs[3:]
    outs, refs = refs[: len(places_out)], refs[len(places_out) :]
    (swished, slope), refs = refs[:2], refs[2:]
    rows_v, gate_v, up_v, down_v, gate_pre, up_pre, swished_v, slope_v, hidden_v, out_v, *sems = refs
    row_sem, gate_sem, up_sem, down_sem, swished_sem, slope_sem, out_sem = sems
    units, width = down.shape
    unit_tiles, column_tiles = tiles(units, FORWARD_TILES[0]), tiles(width, FORWARD_TILES[1])
    loads = []
    for k, part in enumerate(unit_tiles):
        loads.append(
            [
                pltpu.make_async_copy(gate.at[:, part], gate_v.at[:, part], gate_sem.at[k]),
                pltpu.make_async_copy(up.at[:, part], up_v.at[:, part], up_sem.at[k]),
            ]
        )
    for k, part in enumerate(column_tiles):
        loads.append([pltpu.make_async_copy(down.at[:, part], down_v.at[:, part], down_sem.at[k])])
    saves = []

    def activate(k):
        part = unit_tiles[k]
        gates, ups = gate_pre[k % 2], up_pre[k % 2]
        sigmoid_part = jax.nn.sigmoid(gates)
        swish = gates * sigmoid_part
        swished_v[:, part] = swish
        slope_v[:, part] = ups * (sigmoid_part * (1.0 + gates * (1.0 - sigmoid_part)))
        hidden_v[:, part] = (swish * ups).astype(BF16)

    def save(k):
        part = unit_tiles[k]
        copies = [
            pltpu.make_async_copy(swished_v.at[:, part], swished.at[:, part], swished_sem.at[k]),
            pltpu.make_async_copy(slope_v.at[:, part], slope.at[:, part], slope_sem.at[k]),
        ]
        begin(copies)
        saves.extend(copies)

    rows = row_copies(places_in, chunks, rows_v, row_sem)
    begin(rows)
    for k in range(AHEAD):
        begin(loads[k])
    finish_copies(rows)
    for k, part in enumerate(unit_tiles):
        finish_copies(loads[k])
        if k + AHEAD < len(loads):
            begin(loads[k + AHEAD])
        gate_pre[k % 2] = jnp.dot(rows_v[...], gate_v[:, part], preferred_element_type=F32)
        up_pre[k % 2] = jnp.dot(rows_v[...], up_v[:, part], preferred_element_type=F32)
        if k > 0:
            activate(k - 1)
            save(k - 1)
    activate(len(unit_tiles) - 1)
    save(len(unit_tiles) - 1)
    for k, part in enumerate(column_tiles):
        at = len(unit_tiles) + k
        finish_copies(loads[at])
        if at + AHEAD < len(loads):
            begin(loads[at + AHEAD])
        out_v[:, part] = jnp.dot(hidden_v[...], down_v[:, part], preferred_element_type=F32).astype(BF16)
        copies = result_copies(places_out, out_v, part, outs, out_sem.at[k])
        begin(copies)
        saves.extend(copies)
    finish_copies(saves)


def forward(position, chunks, w_gate, w_up, w_down, slots):
    width, units = w_gate.shape
    outs = chunk_shapes(slots, width, False)
    rows = sum(out.shape[0] for out in outs)
    unit_tiles, column_tiles = tiles(units, FORWARD_TILES[0]), tiles(width, FORWARD_TILES[1])
    unit_tile = unit_tiles[0].size
    anywhere = pl.BlockSpec(memory_space=pl.ANY)
    dma = pltpu.SemaphoreType.DMA
    results = pl.pallas_call(
        functools.partial(forward_kernel, slots),
        out_shape=outs + [jax.ShapeDtypeStruct((rows, units), F32)] * 2,
        in_specs=[pl.BlockSpec(memory_space=pltpu.SMEM)] + [anywhere] * (len(chunks) + 3),
        out_specs=[anywhere] * (len(outs) + 2),
        scratch_shapes=[
            pltpu.VMEM((rows, width), BF16),
            pltpu.VMEM((width, units), BF16),
            pltpu.VMEM((width, units), BF16),
            pltpu.VMEM((units, width), BF16),
            pltpu.VMEM((2, rows, unit_tile), F32),
            pltpu.VMEM((2, rows, unit_tile), F32),
            pltpu.VMEM((rows, units), F32),
            pltpu.VMEM((rows, units), F32),
            pltpu.VMEM((rows, units), BF16),
            pltpu.VMEM((rows, width), BF16),
            dma((len(chunks),)),
            dma((len(unit_tiles),)),
            dma((len(unit_tiles),)),
            dma((len(column_tiles),)),
            dma((len(unit_tiles),)),
            dma((len(unit_tiles),)),
            dma((len(column_tiles), len(outs))),
        ],
        compiler_params=pltpu.CompilerParams(vmem_limit_bytes=VMEM_LIMIT),
        cost_estimate=pl.CostEstimate(
            flops=6 * rows * width * units,
            bytes_accessed=6 * width * units + 4 * rows * width + 8 * rows * units,
            transcendentals=rows * units,
        ),
        name="expert_forward",
    )(position, *chunks, w_gate, w_up, w_down)
    return results


def transposed_dot(a, b):
    return lax.dot_general(a, b, (((1,), (1,)), ((), ())), preferred_element_type=F32)


def backward_kernel(slots, pos_ref, *refs):
    places_in, places_out = chunk_places(pos_ref, slots, False), chunk_places(pos_ref, slots, True)
    chunks, refs = refs[: len(places_in)], refs[len(places_in) :]
    (swished, slope, gate, up, down), refs = refs[:5], refs[5:]
    outs, refs = refs[: len(places_out)], refs[len(places_out) :]
    cot_v, gate_v, up_v, down_v, swished_v, slope_v, d_hidden, d_gate, d_up, out_v, *sems = refs
    row_sem, gate_sem, up_sem, down_sem, swished_sem, slope_sem, out_sem = sems
    units, width = down.shape
    unit_tiles, column_tiles = tiles(units, BACKWARD_TILES[0]), tiles(width, BACKWARD_TILES[1])
    loads = []
    for k, part in enumerate(unit_tiles):
        loads.append(
            [
                pltpu.make_async_copy(down.at[part], down_v.at[part], down_sem.at[k]),
                pltpu.make_async_copy(swished.at[:, part], swished_v.at[:, part], swished_sem.at[k]),
                pltpu.make_async_copy(slope.at[:, part], slope_v.at[:, part], slope_sem.at[k]),
            ]
        )
    for k, part in enumerate(column_tiles):
        loads.append(
            [
                pltpu.make_async_copy(gate.at[part], gate_v.at[part], gate_sem.at[k]),
                pltpu.make_async_copy(up.at[part], up_v.at[part], up_sem.at[k]),
            ]
        )
    saves = []

    def activate(k):
        part = unit_tiles[k]
        d_up[:, part] = (d_hidden[k % 2] * swished_v[:, part]).astype(BF16)
        d_gate[:, part] = (d_hidden[k % 2] * slope_v[:, part]).astype(BF16)

    rows = row_copies(places_in, chunks, cot_v, row_sem)
    begin(rows)
    for k in range(AHEAD):
        begin(loads[k])
    finish_copies(rows)
    for k, part in enumerate(unit_tiles):
        finish_copies(loads[k])
        if k + AHEAD < len(loads):
            begin(loads[k + AHEAD])
        d_hidden[k % 2] = transposed_dot(cot_v[...], down_v[part, :])
        if k > 0:
            activate(k - 1)
    activate(len(unit_tiles) - 1)
    for k, part in enumerate(column_tiles):
        at = len(unit_tiles) + k
        finish_copies(loads[at])
        if at + AHEAD < len(loads):
            begin(loads[at + AHEAD])
        out = transposed_dot(d_gate[...], gate_v[part, :]) + transposed_dot(d_up[...], up_v[part, :])
        out_v[:, part] = out.astype(BF16)
        copies = result_copies(places_out, out_v, part, outs, out_sem.at[k])
        begin(copies)
        saves.extend(copies)
    finish_copies(saves)


def backward(position, chunks, swished, slope, w_gate, w_up, w_down, slots):
    width, units = w_gate.shape
    outs = chunk_shapes(slots, width, True)
    rows = sum(out.shape[0] for out in outs)
    unit_tiles, column_tiles = tiles(units, BACKWARD_TILES[0]), tiles(width, BACKWARD_TILES[1])
    anywhere = pl.BlockSpec(memory_space=pl.ANY)
    dma = pltpu.SemaphoreType.DMA
    return pl.pallas_call(
        functools.partial(backward_kernel, slots),
        out_shape=outs,
        in_specs=[pl.BlockSpec(memory_space=pltpu.SMEM)] + [anywhere] * (len(chunks) + 5),
        out_specs=[anywhere] * len(outs),
        scratch_shapes=[
            pltpu.VMEM((rows, width), BF16),
            pltpu.VMEM((width, units), BF16),
            pltpu.VMEM((width, units), BF16),
            pltpu.VMEM((units, width), BF16),
            pltpu.VMEM((rows, units), F32),
            pltpu.VMEM((rows, units), F32),
            pltpu.VMEM((2, rows, unit_tiles[0].size), F32),
            pltpu.VMEM((rows, units), BF16),
            pltpu.VMEM((rows, units), BF16),
            pltpu.VMEM((rows, width), BF16),
            dma((len(chunks),)),
            dma((len(column_tiles),)),
            dma((len(column_tiles),)),
            dma((len(unit_tiles),)),
            dma((len(unit_tiles),)),
            dma((len(unit_tiles),)),
            dma((len(column_tiles), len(outs))),
        ],
        compiler_params=pltpu.CompilerParams(vmem_limit_bytes=VMEM_LIMIT),
        cost_estimate=pl.CostEstimate(
            flops=6 * rows * width * units,
            bytes_accessed=6 * width * units + 4 * rows * width + 8 * rows * units,
            transcendentals=0,
        ),
        name="expert_backward",
    )(position, *chunks, swished, slope, w_gate, w_up, w_down)


def sum_kernel(pos_ref, own_ref, *refs):
    parts, out_ref = refs[:-1], refs[-1]
    size = own_ref.shape[0]
    total = jnp.zeros(own_ref.shape, F32)
    for part in parts:
        for start in range(0, part.shape[0], size):
            total = total + part[start : start + size, :].astype(F32)
    y_lo = pos_ref[1]
    out_ref[pl.ds(pl.multiple_of(y_lo * size, size), size), :] = own_ref[...]
    out_ref[pl.ds(pl.multiple_of((1 - y_lo) * size, size), size), :] = total.astype(BF16)


def sum_quarters(position, parts, own):
    rows, width = own.shape
    vmem = pl.BlockSpec(memory_space=pltpu.VMEM)
    return pl.pallas_call(
        sum_kernel,
        out_shape=jax.ShapeDtypeStruct((2 * rows, width), BF16),
        in_specs=[pl.BlockSpec(memory_space=pltpu.SMEM)] + [vmem] * (1 + len(parts)),
        out_specs=vmem,
        compiler_params=pltpu.CompilerParams(vmem_limit_bytes=VMEM_LIMIT),
        cost_estimate=pl.CostEstimate(
            flops=4 * rows * width, bytes_accessed=14 * rows * width, transcendentals=0
        ),
        name="sum_quarters",
    )(position, own, *parts)


def combine_hits(slots, pos_ref, meta):
    count = meta.shape[0]
    target = slot_targets(pos_ref, lax.broadcasted_iota(jnp.int32, (count, 6 * slots), 1), slots).astype(F32)
    return (target == meta[:, 0:1]).astype(F32), (target == meta[:, 1:2]).astype(F32)


def returned_rows(refs, columns, blank):
    return jnp.concatenate([ref[:, columns] for ref in refs] + [jnp.zeros(blank, BF16)], axis=0)


def combine_out_kernel(slots, pos_ref, meta_ref, upstream_ref, *refs):
    returned, (out_ref, dots_ref) = refs[:-2], refs[-2:]
    count, width = upstream_ref.shape
    meta = meta_ref[...]
    hit0, hit1 = [hit.astype(BF16) for hit in combine_hits(slots, pos_ref, meta)]
    tile = column_tile(width)
    dots0 = dots1 = jnp.zeros((count, 1), F32)
    for start in range(0, width, tile):
        columns = slice(start, start + tile)
        terms = returned_rows(returned, columns, (slots, tile))
        rows0 = jnp.dot(hit0, terms, preferred_element_type=F32)
        rows1 = jnp.dot(hit1, terms, preferred_element_type=F32)
        out_ref[:, columns] = (meta[:, 2:3] * rows0 + meta[:, 3:4] * rows1).astype(BF16)
        upstream = upstream_ref[:, columns].astype(F32)
        dots0 = dots0 + jnp.sum(upstream * rows0, axis=1, keepdims=True)
        dots1 = dots1 + jnp.sum(upstream * rows1, axis=1, keepdims=True)
    lane = lax.broadcasted_iota(jnp.int32, dots_ref.shape, 1)
    high0, high1 = dots0.astype(BF16).astype(F32), dots1.astype(BF16).astype(F32)
    extra = jnp.where(lane == 0, high0, 0.0)
    extra = jnp.where(lane == 1, dots0 - high0, extra)
    extra = jnp.where(lane == 2, high1, extra)
    extra = jnp.where(lane == 3, dots1 - high1, extra)
    dots_ref[...] = extra.astype(BF16)


def combine_out(position, meta, upstream, returned, slots):
    count, width = upstream.shape
    vmem = pl.BlockSpec(memory_space=pltpu.VMEM)
    return pl.pallas_call(
        functools.partial(combine_out_kernel, slots),
        out_shape=[jax.ShapeDtypeStruct((count, size), BF16) for size in (width, 128)],
        in_specs=[pl.BlockSpec(memory_space=pltpu.SMEM)] + [vmem] * (3 + SIDE),
        out_specs=[vmem] * 2,
        compiler_params=pltpu.CompilerParams(vmem_limit_bytes=VMEM_LIMIT),
        cost_estimate=pl.CostEstimate(
            flops=4 * count * 6 * slots * width, bytes_accessed=10 * slots * width + 4 * count * width, transcendentals=0
        ),
        name="combine_out",
    )(position, meta, upstream, *returned)


def combine_grad_kernel(slots, pos_ref, meta_ref, out_terms_ref, dots_ref, *refs):
    returned, out_ref = refs[:-1], refs[-1]
    width = returned[0].shape[1]
    hit0, hit1 = combine_hits(slots, pos_ref, meta_ref[...])
    both = (hit0 + hit1).astype(BF16)
    tile = column_tile(width)
    for start in range(0, width, tile):
        columns = slice(start, start + tile)
        terms = returned_rows(returned, columns, (slots, tile))
        out_ref[:, columns] = out_terms_ref[:, columns]
        grads = jnp.dot(both, terms, preferred_element_type=F32)
        out_ref[:, width + start : width + start + tile] = grads.astype(BF16)
    out_ref[:, 2 * width :] = dots_ref[...]


def combine_grad(position, meta, out_terms, dots, returned, slots):
    count, width = out_terms.shape
    vmem = pl.BlockSpec(memory_space=pltpu.VMEM)
    return pl.pallas_call(
        functools.partial(combine_grad_kernel, slots),
        out_shape=jax.ShapeDtypeStruct((count, 2 * width + dots.shape[1]), BF16),
        in_specs=[pl.BlockSpec(memory_space=pltpu.SMEM)] + [vmem] * (4 + SIDE),
        out_specs=vmem,
        compiler_params=pltpu.CompilerParams(vmem_limit_bytes=VMEM_LIMIT),
        cost_estimate=pl.CostEstimate(
            flops=2 * count * 6 * slots * width, bytes_accessed=10 * slots * width + 6 * count * width, transcendentals=0
        ),
        name="combine_grad",
    )(position, meta, out_terms, dots, *returned)


def finish_kernel(slots, pos_ref, meta_ref, router_ref, parts_ref, layer_ref, rows_ref):
    share, width = layer_ref.shape
    sums = parts_ref[0:share, :].astype(F32)
    for k in range(1, parts_ref.shape[0] // share):
        sums = sums + parts_ref[k * share : (k + 1) * share, :].astype(F32)
    layer_ref[...] = sums[:, :width].astype(BF16)
    grads, extra = sums[:, width : 2 * width], sums[:, 2 * width :]
    d_gap = (extra[:, 0:1] + extra[:, 1:2]) - (extra[:, 2:3] + extra[:, 3:4])
    meta = meta_ref[pl.ds(pl.multiple_of(pos_ref[4] * share, share), share), :]
    d_left = meta[:, 2:3] * meta[:, 3:4] * d_gap
    d_left = d_left.astype(BF16).astype(F32)
    chosen = meta.astype(jnp.int32) // slots
    router = router_ref[...].astype(F32)
    for e in range(router.shape[0]):
        sign = (chosen[:, 0:1] == e).astype(F32) - (chosen[:, 1:2] == e).astype(F32)
        grads = grads + (sign * d_left) * router[e : e + 1, :]
    rows_ref[...] = grads.astype(BF16)


def finish(position, meta, router, parts, share, slots):
    width = router.shape[1]
    vmem = pl.BlockSpec(memory_space=pltpu.VMEM)
    return pl.pallas_call(
        functools.partial(finish_kernel, slots),
        out_shape=[jax.ShapeDtypeStruct((share, width), BF16)] * 2,
        in_specs=[pl.BlockSpec(memory_space=pltpu.SMEM)] + [vmem] * 3,
        out_specs=[vmem] * 2,
        compiler_params=pltpu.CompilerParams(vmem_limit_bytes=VMEM_LIMIT),
        cost_estimate=pl.CostEstimate(
            flops=30 * parts.shape[0] * width, bytes_accessed=5 * parts.shape[0] * width, transcendentals=0
        ),
        name="finish",
    )(position, meta, router, parts)


def along(axis, sign, chunks):
    return [chunk if by == 0 else moved(chunk, axis, sign * by) for chunk, by in zip(chunks, STEPS)]


def halves(position, head, slots):
    y_lo = position[1]
    return [lax.dynamic_slice_in_dim(head, half * slots, slots, 0) for half in (y_lo, 1 - y_lo)]


def per_device(
    tokens_in, cotangent_in, expert_ids, router_weight, gate_weight, up_weight, down_weight
):
    swap = [(0, 1), (1, 0)]
    arrived = lax.ppermute(tokens_in[0], "pipe", swap)
    upstream = lax.ppermute(cotangent_in[0], "pipe", swap)
    routes = expert_ids[0].T
    router = router_weight[0].T
    w_gate = gate_weight[0, 0]
    w_up = up_weight[0, 0]
    w_down = down_weight[0, 0]
    count = arrived.shape[0]
    slots = 4 * count // lax.axis_size("expert")
    group = lax.axis_index("expert")
    part = lax.axis_index("etp")
    position = jnp.stack([group, group // SIDE, group % SIDE, part % SIDE, part]).astype(jnp.int32)
    plan, hits = plan_slots(position, routes, count, slots)
    rows_head, *rows = dispatch_rows(hits, arrived, slots)
    rows_head = exchange(rows_head, "expert")
    *rows, rows_far = [rows[by] for by in STEPS]
    rows = along("expert", 1, rows)
    meta, cot_head, *cot = dispatch_cot(position, plan, arrived, upstream, router, slots)
    rows_head, rows = lax.optimization_barrier((rows_head, rows))
    own, quarter = halves(position, rows_head, slots)
    quarters = along("etp", 1, [quarter] * SIDE)
    rows_far = moved(rows_far, "expert", STEPS[-1])
    cot_head = exchange(cot_head, "expert")
    cot_far = moved(cot[STEPS[-1]], "expert", STEPS[-1])
    rows_far, cot_far, quarters, cot_head, cot = lax.optimization_barrier((rows_far, cot_far, quarters, cot_head, cot))
    chunks = (*rows, rows_far, own, *quarters)
    own, quarter = halves(position, cot_head, slots)
    quarters = exchange(jnp.broadcast_to(quarter[None], (SIDE, *quarter.shape)).reshape(SIDE * slots, -1), "etp", low=True)
    cot = [*along("expert", 1, [cot[by] for by in STEPS[:-1]]), cot_far]
    *out, own_out, out_quarters, swished, slope = forward(position, chunks, w_gate, w_up, w_down, slots)
    out_quarters = exchange(out_quarters, "etp", low=True)
    out = along("expert", -1, out)
    grad = backward(position, (*cot, own, quarters), swished, slope, w_gate, w_up, w_down, slots)
    out_quarters, out, grad = lax.optimization_barrier((out_quarters, out, grad))
    grad, own_grad, grad_quarters = grad[:SIDE], grad[SIDE], grad[1 + SIDE :]
    grad_quarters = along("etp", -1, grad_quarters)
    grad = along("expert", -1, grad)
    in_order = lambda head, chunks: [head] + [chunks[STEPS.index(by)] for by in range(SIDE)]
    out_head = exchange(sum_quarters(position, [out_quarters], own_out), "expert")
    grad_quarters, grad, out_head = lax.optimization_barrier((grad_quarters, grad, out_head))
    out_terms, dots = combine_out(position, meta, upstream, in_order(out_head, out), slots)
    grad_head = exchange(sum_quarters(position, grad_quarters, own_grad), "expert")
    terms = combine_grad(position, meta, out_terms, dots, in_order(grad_head, grad), slots)
    share = count // lax.axis_size("etp")
    layer_rows, grad_rows = finish(position, meta, router, exchange(terms, "etp"), share, slots)
    return (layer_rows[None], grad_rows[None])


def solution(mesh):
    return jax.shard_map(
        per_device,
        mesh=mesh,
        in_specs=(
            P("pipe", "expert", None),
            P("pipe", "expert", None),
            P("pipe", None, None),
            P("pipe", None, None),
            P("pipe", "expert", None, "etp"),
            P("pipe", "expert", None, "etp"),
            P("pipe", "expert", "etp", None),
        ),
        out_specs=(P("pipe", ("expert", "etp"), None), P("pipe", ("expert", "etp"), None)),
        check_vma=False,
    )
```
